128 devices in a mesh: node: 16 (over y, x), local: 8 (over z, core).
Axes of the slice: x: 4, y: 4, z: 4, core: 2. Of those that a mesh axis runs over, the one named last changes fastest.
Arguments:
- hidden_in: bfloat16 [1024, 7168], P(('node', 'local')), may hold values from -6 to 6
- expert_ids: int32 [1024, 8], P(('node', 'local')), may hold values from 0 to 31, all different within a row; in each aligned block of 64 rows (0 to 63, 64 to 127, ...) at most 24 rows name the same one
- affinity: bfloat16 [1024, 8], P(('node', 'local')), may hold values from 0.049804688 to 1
- norm_gain: float32 [7168], replicated, may hold values from 0.5 to 1.5
- gate_w: bfloat16 [128, 7168, 512], P(('node', 'local')), may hold values from -0.0625 to 0.0625
- up_w: bfloat16 [128, 7168, 512], P(('node', 'local')), may hold values from -0.0625 to 0.0625
- down_w: bfloat16 [32, 2048, 7168], P('node', None, 'local'), may hold values from -0.125 to 0.125
- shared_gate: bfloat16 [7168, 2048], P(None, 'local'), may hold values from -0.0625 to 0.0625
- shared_up: bfloat16 [7168, 2048], P(None, 'local'), may hold values from -0.0625 to 0.0625
- shared_down: bfloat16 [2048, 7168], P(None, 'local'), may hold values from -0.125 to 0.125
Outputs:
- block_out: bfloat16 [1024, 7168], P('node', 'local')
The draws below stay inside these ranges and needn't reach their ends.
Inputs may be any that keep to these rules, and one draw needn't show every extreme that they name: `expert_ids`: each token names 8 different experts; in each aligned block of 64 tokens no expert is named more than 24 times, a bound that some block reaches.
All inputs are finite; a program needn't handle non-finite values.
Results may differ from the reference program's by a relative error of at most 0.0055.
Values may be sent and summed in bfloat16 or wider, within the bound.
A program may use at most 128 MiB of HBM per device.

```python
import math
import jax
import jax.numpy as jnp
import numpy as np
from jax import lax

D = 7168
FF = 2048
TOP = 8
TOK_DEV = 8
EXPERTS = 32
HPARTS = 4
CAP = 24
TOKENS = 1024
N_NODE = 16
N_LOCAL = 8


def levels(rng, dims, pieces, low, top_value):
    def one(position, shards_of):
        heights = jax.random.uniform(jax.random.fold_in(jax.random.fold_in(rng, 6), position), (shards_of,), jnp.float32, low / len(pieces), top_value / len(pieces))
        return jnp.repeat(jnp.exp(heights), dims[position] // shards_of).reshape((-1,) + (1,) * (len(dims) - position - 1))

    gain = one(*pieces[0])
    for cut in pieces[1:]:
        gain = gain * one(*cut)
    return gain


def routed_block(stream_key, own, number, rows, count, top, limit, slope):
    order = jax.random.permutation(stream_key, count)
    crowded, common = shares(count, rows * top, limit, slope, True), shares(count, rows * top, limit, slope, False)
    places = jnp.arange(count)

    def named(lengths, turn):
        used = int((lengths > 0).sum())
        fixed = max(1, used // 4)
        shifted = fixed + (places - fixed + turn * (used - fixed)) % max(1, count - fixed)
        return jnp.zeros((count,), jnp.int32).at[order[jnp.where(places < fixed, places, shifted)]].set(jnp.asarray(lengths, jnp.int32))

    lengths = jnp.where(number % 4 == 0, named(crowded, number // 4), named(common, number - number // 4 - 1))
    mixed = jax.random.permutation(jax.random.fold_in(own, 3), count)
    donor, receiver = mixed[0:count // 2 * 2:2], mixed[1:count // 2 * 2:2]
    margin = jnp.minimum(lengths[donor] - 1, limit - lengths[receiver]) // 2
    margin = jnp.where((donor == order[0]) | (receiver == order[0]) | (lengths[receiver] == 0), 0, jnp.maximum(margin, 0))
    shifted = jax.random.randint(jax.random.fold_in(own, 4), (count // 2,), 0, 1 << 20) % (margin + 1)
    lengths = lengths.at[donor].add(-shifted).at[receiver].add(shifted)
    items = jnp.searchsorted(jnp.cumsum(lengths), jnp.arange(rows * top), side="right").astype(jnp.int32)
    listing = items.reshape(top, rows).T
    listing = listing[jax.random.permutation(jax.random.fold_in(own, 1), rows)]
    turn = jax.random.randint(jax.random.fold_in(own, 2), (rows, 1), 0, top)
    return jnp.take_along_axis(listing, (jnp.arange(top)[None, :] + turn) % top, axis=1)


def shares(amount, total, limit, slope, full):
    portions = [(1 << 20) // math.isqrt(standing ** slope) + 1 for standing in range(1, amount + 1)]
    largest = limit if full else min(limit, max(-(-total // amount), total * portions[0] // sum(portions)))
    least = 1 if total - largest >= amount - 1 else 0
    given, surplus = [largest] + [least] * (amount - 1), total - largest - least * (amount - 1)
    while surplus > 0:
        movable = [i for i in range(1, amount) if given[i] < largest] or [i for i in range(1, amount) if given[i] < limit]
        pool, left = sum([portions[i] for i in movable]), surplus
        for i in movable:
            extra = min(limit - given[i], max(1, left * portions[i] // pool), surplus)
            given[i] = given[i] + extra
            surplus = surplus - extra
    return np.array(given)


def gaussian(stream_key, shape, spread, limit, split=(), held_as=jnp.bfloat16):
    array = spread * jax.random.normal(stream_key, shape, jnp.float32)
    if split:
        array = array * levels(stream_key, shape, split, -0.22, 0.18)
    return jnp.clip(array, -limit, limit).astype(held_as)


def setup_inputs(seed: int = 0) -> dict:
    key_list = jax.random.split(jax.random.key(seed), 11)
    hidden_in = gaussian(key_list[0], (TOKENS, D), 1.0, 6.0, ((0, 128),))
    expert_ids_keys = jax.random.split(jax.random.fold_in(key_list[1], 1), TOKENS // (TOK_DEV * N_LOCAL))
    expert_ids_turns = jax.random.permutation(jax.random.fold_in(key_list[1], 3), TOKENS // (TOK_DEV * N_LOCAL))
    expert_ids = jax.vmap(lambda own, number: routed_block(jax.random.fold_in(key_list[1], 2), own, number, TOK_DEV * N_LOCAL, EXPERTS, TOP, CAP, 1))(expert_ids_keys, expert_ids_turns).reshape((TOKENS, TOP))
    affinity = jnp.clip(jnp.exp(math.log(1.0) - 2.9996462 * jax.random.uniform(key_list[2], (TOKENS, TOP), jnp.float32) ** levels(key_list[2], (TOKENS, TOP), ((0, 128),), -0.2, 0.2)), 0.049804688, 1.0).astype(jnp.bfloat16)
    norm_gain = jnp.clip(jax.random.uniform(key_list[3], (D,), jnp.float32, 0.5, 1.5), 0.5, 1.5)
    gate_w = gaussian(key_list[4], (EXPERTS * HPARTS, D, FF // HPARTS), D ** -0.5, 0.0625, ((0, 128),))
    up_w = gaussian(key_list[5], (EXPERTS * HPARTS, D, FF // HPARTS), D ** -0.5, 0.0625, ((0, 128),))
    down_w = gaussian(key_list[6], (EXPERTS, FF, D), FF ** -0.5, 0.125, ((0, 16), (2, 8)))
    shared_gate = gaussian(key_list[7], (D, FF), D ** -0.5, 0.0625, ((1, 8),))
    shared_up = gaussian(key_list[8], (D, FF), D ** -0.5, 0.0625, ((1, 8),))
    shared_down = gaussian(key_list[9], (FF, D), FF ** -0.5, 0.125, ((1, 8),))
    return {"hidden_in": hidden_in, "expert_ids": expert_ids, "affinity": affinity, "norm_gain": norm_gain, "gate_w": gate_w, "up_w": up_w, "down_w": down_w, "shared_gate": shared_gate, "shared_up": shared_up, "shared_down": shared_down}


def run_expert(inputs):
    rows, gate_parts, up_parts, w_down = inputs
    w_gate = gate_parts.transpose(1, 0, 2).reshape(D, FF)
    w_up = up_parts.transpose(1, 0, 2).reshape(D, FF)
    gate = jnp.dot(rows, w_gate, preferred_element_type=jnp.float32)
    upper = jnp.dot(rows, w_up, preferred_element_type=jnp.float32)
    act = (jax.nn.silu(gate) * upper).astype(jnp.bfloat16)
    return jnp.dot(act, w_down, preferred_element_type=jnp.float32).astype(jnp.bfloat16)

def reference(hidden_in, expert_ids, affinity, norm_gain, gate_w, up_w, down_w, shared_gate, shared_up, shared_down):
    values = hidden_in.astype(jnp.float32)
    scale = lax.rsqrt(lax.optimization_barrier(jnp.mean(values * values, axis=-1, keepdims=True)) + 1e-06)
    normed = (values * scale * norm_gain).astype(jnp.bfloat16)
    block_rows = TOK_DEV * N_LOCAL
    flat_ids = expert_ids.reshape(N_NODE, block_rows * TOP)
    onehot = (flat_ids[:, :, None] == jnp.arange(EXPERTS, dtype=jnp.int32)[None, None, :]).astype(jnp.int32)
    before = jnp.cumsum(onehot, axis=1) - onehot
    slot_index = lax.optimization_barrier(jnp.sum(before * onehot, axis=-1))
    target = flat_ids * CAP + slot_index
    row_of = jnp.arange(block_rows * TOP, dtype=jnp.int32) // TOP
    spread_rows = normed.reshape(N_NODE, block_rows, D)[:, row_of]
    node_index = jnp.arange(N_NODE, dtype=jnp.int32)[:, None]
    buffer = jnp.zeros((N_NODE, EXPERTS * CAP, D), jnp.bfloat16).at[node_index, target].set(spread_rows)
    expert_rows = buffer.reshape(N_NODE, EXPERTS, CAP, D).transpose(1, 0, 2, 3).reshape(EXPERTS, N_NODE * CAP, D)
    part_width = FF // HPARTS
    gate_parts = gate_w.reshape(EXPERTS, HPARTS, D, part_width)
    up_parts = up_w.reshape(EXPERTS, HPARTS, D, part_width)
    outputs = lax.map(run_expert, (expert_rows, gate_parts, up_parts, down_w))
    returned = outputs.reshape(EXPERTS, N_NODE, CAP, D).transpose(1, 0, 2, 3).reshape(N_NODE, EXPERTS * CAP, D)
    picked = returned[node_index, target].reshape(TOKENS, TOP, D).astype(jnp.float32)
    weight_in = affinity.astype(jnp.float32)
    mix = 2.5 * weight_in / lax.optimization_barrier(jnp.sum(weight_in, axis=-1, keepdims=True))
    routed = lax.optimization_barrier(jnp.sum(mix[:, :, None] * picked, axis=1))
    shared_g = jnp.dot(normed, shared_gate, preferred_element_type=jnp.float32)
    shared_u = jnp.dot(normed, shared_up, preferred_element_type=jnp.float32)
    shared_act = (jax.nn.silu(shared_g) * shared_u).astype(jnp.bfloat16)
    shared_out = jnp.dot(shared_act, shared_down, preferred_element_type=jnp.float32)
    return (values + shared_out + routed).astype(jnp.bfloat16)
```

```python
import functools

import jax
import jax.numpy as jnp
from jax import lax
from jax.experimental import pallas as pl
from jax.experimental.pallas import tpu as pltpu
from jax.sharding import PartitionSpec as P

MESH = pl.DeviceIdType.MESH
F32 = jnp.float32
BF16 = jnp.bfloat16
RING = 4
META = 128
CAP = 24
TOP = 8


def remote(src, dst, send, recv, device):
    return pltpu.make_async_remote_copy(
        src_ref=src,
        dst_ref=dst,
        send_sem=send,
        recv_sem=recv,
        device_id=device,
        device_id_type=MESH,
    )


def dot(a, b):
    return jnp.dot(a, b, preferred_element_type=F32)


class Gather:
    def __init__(self, slot, first, second, pos, plus, minus, send, recv, other=None):
        self.slot, self.first, self.second = slot, first, second
        self.pos, self.plus, self.minus, self.other = pos, plus, minus, other
        self.send, self.recv = send, recv
        self.before = lax.rem(pos + RING - 1, RING)
        self.after = lax.rem(pos + 1, RING)
        self.far = lax.rem(pos + 2, RING)
        self.sent = []

    def copy(self, ref, index, device):
        return remote(ref, ref, self.send.at[index], self.recv.at[index], device)

    def go(self, ref, index, device):
        copy = self.copy(ref, index, device)
        copy.start()
        self.sent.append(copy)

    def share(self, place, index):
        if self.other is not None:
            self.go(self.slot(place), index, self.other)

    def start(self):
        self.go(self.slot(self.pos), 0, self.plus)
        self.go(self.slot(self.pos), 1, self.minus)
        self.share(self.pos, 4)

    def pass_on(self):
        self.copy(self.slot(self.before), 0, self.plus).wait_recv()
        self.go(self.first(self.before), 2, self.plus)
        self.copy(self.slot(self.after), 1, self.minus).wait_recv()
        self.go(self.second(self.after), 3, self.minus)
        self.share(self.before, 5)
        self.share(self.after, 6)

    def finish(self):
        self.copy(self.first(self.far), 2, self.plus).wait_recv()
        self.copy(self.second(self.far), 3, self.minus).wait_recv()
        self.share(self.far, 7)

    def shared(self, mirror):
        for place, index in ((self.pos, 4), (self.before, 5), (self.after, 6), (self.far, 7)):
            self.copy(mirror(place), index, self.other).wait_recv()

    def drain(self):
        for copy in self.sent:
            copy.wait_send()
        self.sent = []


def kernel(
    hid,
    ids,
    aff,
    gain,
    gate_hbm,
    up_hbm,
    down_hbm,
    sgate_hbm,
    sup_hbm,
    sdown_hbm,
    out,
    wg,
    wu,
    wd,
    sg,
    su,
    sd,
    pair_out,
    pair_in,
    zh,
    xa,
    xo,
    ct,
    cs,
    fw,
    rh,
    ac,
    sa,
    sres,
    oo,
    pp,
    r1,
    r2,
    t1,
    r3,
    r4,
    wsem,
    bsem,
    zsend,
    zrecv,
    asend,
    arecv,
    ssend,
    srecv,
    csend,
    crecv,
    gsend,
    grecv,
    rsend,
    rrecv,
):
    half = hid.shape[1] // 2
    node, local = lax.axis_index("node"), lax.axis_index("local")
    y, x = node // RING, lax.rem(node, RING)
    z, c = local // 2, lax.rem(local, 2)
    d = 1 - c
    up1 = lambda v: lax.rem(v + 1, RING)
    dn1 = lambda v: lax.rem(v + RING - 1, RING)
    sib = (node, z * 2 + d)
    z_plus, z_minus = (node, up1(z) * 2 + c), (node, dn1(z) * 2 + c)
    x_plus, x_minus = (y * RING + up1(x), local), (y * RING + dn1(x), local)
    y_plus, y_minus = (up1(y) * RING + x, local), (dn1(y) * RING + x, local)
    a_plus = (d * y_plus[0] + c * x_plus[0], local)
    a_minus = (d * y_minus[0] + c * x_minus[0], local)
    b_plus = (d * x_plus[0] + c * y_plus[0], local)
    b_minus = (d * x_minus[0] + c * y_minus[0], local)
    apos, bpos = d * y + c * x, d * x + c * y

    barrier = pltpu.get_barrier_semaphore()
    for peer in (sib, z_plus, z_minus, x_plus, x_minus, y_plus, y_minus):
        pl.semaphore_signal(barrier, inc=1, device_id=peer, device_id_type=MESH)

    values = hid[...].astype(F32)
    scale = lax.rsqrt(jnp.mean(values * values, axis=-1, keepdims=True) + 1e-06)
    s_hi = scale.astype(BF16).astype(F32)
    s_mid = (scale - s_hi).astype(BF16).astype(F32)
    s_lo = scale - s_hi - s_mid
    weight = aff[...].astype(F32)
    mix = 2.5 * weight / jnp.sum(weight, axis=-1, keepdims=True)
    m_hi = mix.astype(BF16).astype(F32)
    m_lo = mix - m_hi
    named = ids[...].astype(F32)
    rows = hid.shape[0]
    lane = lax.broadcasted_iota(jnp.int32, (rows, META), 1)
    place = (z * 2 * rows + c * rows + lax.broadcasted_iota(jnp.int32, (rows, META), 0)).astype(F32)
    meta = jnp.where(lane == 16, place, 0.0)
    meta = jnp.where(lane == 17, 1.0, meta)
    meta = jnp.where(lane == 18, s_hi, meta)
    meta = jnp.where(lane == 19, s_mid, meta)
    meta = jnp.where(lane == 20, s_lo, meta)
    for k in range(TOP):
        meta = jnp.where(lane == k, named[:, k : k + 1], meta)
        meta = jnp.where(lane == 8 + k, m_hi[:, k : k + 1], meta)
        meta = jnp.where(lane == 24 + k, m_lo[:, k : k + 1], meta)
    other_cols = pl.ds(pl.multiple_of(d * half, 128), half)
    own_cols = pl.ds(pl.multiple_of(c * half, 128), half)
    pair_out[:, :half] = hid[:, other_cols].astype(F32)
    pair_out[:, half:] = meta

    pl.semaphore_wait(barrier, 7)
    pair = remote(pair_out, pair_in, bsem.at[0], bsem.at[1], sib)
    pair.start()
    loads = [
        pltpu.make_async_copy(src, dst, wsem.at[i])
        for i, (src, dst) in enumerate(
            (
                (sgate_hbm, sg),
                (sup_hbm, su),
                (gate_hbm.at[0], wg),
                (up_hbm.at[0], wu),
                (sdown_hbm, sd),
                (down_hbm, wd),
            )
        )
    ]
    for load in loads:
        load.start()
    own = jnp.concatenate([hid[:, own_cols].astype(F32), meta], axis=1)
    pair.wait()
    theirs = pair_in[...]
    zh[c, z] = jnp.concatenate(
        [jnp.where(c == 0, own, theirs), jnp.where(c == 0, theirs, own)], axis=0
    ).astype(BF16)

    cut = 15 * 128
    zg = Gather(
        lambda q: zh.at[c, q],
        lambda q: zh.at[c, q, :, pl.ds(0, cut)],
        lambda q: zh.at[c, q, :, pl.ds(cut, half + META - cut)],
        z,
        z_plus,
        z_minus,
        zsend,
        zrecv,
        sib,
    )
    zg.start()
    zg.pass_on()
    zg.finish()

    block = RING * zh.shape[2]

    def normed(h):
        held = zh[h].reshape(block, half + META)
        info = held[:, half:].astype(F32)
        by = info[:, 18:19] + info[:, 19:20] + info[:, 20:21]
        return (held[:, :half].astype(F32) * by * gain[h]).astype(BF16)

    xa[apos, :, :half] = normed(c)
    xa[apos, :, half:] = zh[c, :, :, half:].reshape(block, META)
    part = block // 2
    ag = Gather(
        lambda q: xa.at[q],
        lambda q: xa.at[q, pl.ds(0, part)],
        lambda q: xa.at[q, pl.ds(part, part)],
        apos,
        a_plus,
        a_minus,
        asend,
        arecv,
    )
    ag.start()
    zg.shared(lambda q: zh.at[d, q])
    xo[...] = normed(d)

    loads[0].wait()
    loads[1].wait()
    own_rows = pl.ds(pl.multiple_of(c * half, 128), half)
    other_rows = pl.ds(pl.multiple_of(d * half, 128), half)
    mine = xa[apos, :, :half]
    s_gate = dot(mine, sg[own_rows, :]) + dot(xo[...], sg[other_rows, :])
    s_up = dot(mine, su[own_rows, :]) + dot(xo[...], su[other_rows, :])
    sa[c, z] = (s_gate / (1.0 + jnp.exp(-s_gate)) * s_up).astype(BF16)
    hrow = sa.shape[2] // 2
    sh = Gather(
        lambda q: sa.at[c, q],
        lambda q: sa.at[c, q, pl.ds(0, hrow)],
        lambda q: sa.at[c, q, pl.ds(hrow, hrow)],
        z,
        z_plus,
        z_minus,
        ssend,
        srecv,
        sib,
    )
    sh.start()
    ag.pass_on()
    sh.pass_on()
    ag.finish()

    tokens = RING * block
    info = xa[:, :, half:].reshape(tokens, META).astype(F32)
    lane = lax.broadcasted_iota(jnp.int32, (tokens, META), 1).astype(F32)
    names = jnp.zeros((tokens, META), F32)
    for k in range(TOP):
        names = jnp.where(info[:, k : k + 1] == lane, 1.0, names)
    t_row = lax.broadcasted_iota(jnp.int32, (tokens, tokens), 0)
    t_col = lax.broadcasted_iota(jnp.int32, (tokens, tokens), 1)
    earlier = jnp.where((t_col < t_row) & (t_col // block == t_row // block), 1.0, 0.0)
    counts = dot(earlier.astype(BF16), names.astype(BF16))
    base = (lax.broadcasted_iota(jnp.int32, (tokens, META), 0) // block * CAP).astype(F32)
    ct[...] = jnp.where(names > 0.5, counts + base, -1.0).T

    group = RING * CAP
    tile = 256
    tiles = half // tile
    slot_no = lax.broadcasted_iota(jnp.int32, (group, tokens), 0).astype(F32)

    def pick(step, dest):
        there = lax.rem(bpos + step, RING)
        expert = (d * (y * RING + there) + c * (there * RING + x)) * 2 + z // 2
        chosen = jnp.where(ct[pl.ds(expert, 1), :] == slot_no, 1.0, 0.0).astype(BF16)

        @pl.loop(0, tiles)
        def _(j):
            cols = pl.ds(pl.multiple_of(j * tile, tile), tile)
            dest[:, cols] = dot(chosen, xa[:, :, cols].reshape(tokens, tile)).astype(BF16)

        dest[:, half:] = dot(chosen, xa[:, :, half:].reshape(tokens, META)).astype(BF16)

    b_prev, b_next = dn1(bpos), up1(bpos)
    b_far = up1(b_next)
    gh = group // 2
    pick(2, cs.at[1])
    routed = [
        remote(cs.at[1, pl.ds(0, gh)], fw.at[0], csend.at[0], crecv.at[0], b_plus),
        remote(cs.at[1, pl.ds(gh, gh)], fw.at[1], csend.at[1], crecv.at[1], b_minus),
    ]
    routed[0].start()
    routed[1].start()
    pick(1, cs.at[0])
    routed.append(remote(cs.at[0], rh.at[c, bpos], csend.at[2], crecv.at[2], b_plus))
    routed[2].start()
    pick(3, cs.at[2])
    routed.append(remote(cs.at[2], rh.at[c, bpos], csend.at[3], crecv.at[3], b_minus))
    routed[3].start()
    pick(0, rh.at[c, bpos])

    def both(q, index):
        copy = remote(rh.at[c, q], rh.at[c, q], csend.at[index], crecv.at[index], sib)
        copy.start()
        routed.append(copy)

    both(bpos, 6)
    sh.finish()
    sh.shared(lambda q: sa.at[d, q])
    loads[4].wait()
    total = jnp.zeros(sres.shape, F32)
    wide = sa.shape[3]
    for zz in range(RING):
        for cc in range(2):
            total += dot(sa[cc, zz], sd[(zz * 2 + cc) * wide : (zz * 2 + cc + 1) * wide, :])
    sres[...] = total

    routed[0].wait_recv()
    onward = remote(
        fw.at[0], rh.at[c, b_prev, pl.ds(0, gh)], csend.at[4], crecv.at[4], b_plus
    )
    onward.start()
    routed.append(onward)
    routed[1].wait_recv()
    onward = remote(
        fw.at[1], rh.at[c, b_next, pl.ds(gh, gh)], csend.at[5], crecv.at[5], b_minus
    )
    onward.start()
    routed.append(onward)
    remote(cs.at[0], rh.at[c, b_prev], csend.at[2], crecv.at[2], b_plus).wait_recv()
    both(b_prev, 7)
    remote(cs.at[2], rh.at[c, b_next], csend.at[3], crecv.at[3], b_minus).wait_recv()
    both(b_next, 8)
    remote(
        fw.at[0], rh.at[c, b_far, pl.ds(0, gh)], csend.at[4], crecv.at[4], b_plus
    ).wait_recv()
    remote(
        fw.at[1], rh.at[c, b_far, pl.ds(gh, gh)], csend.at[5], crecv.at[5], b_minus
    ).wait_recv()
    both(b_far, 9)
    o_prev, o_next = dn1(apos), up1(apos)
    o_far = up1(o_next)
    for q, index in ((apos, 6), (o_prev, 7), (o_next, 8), (o_far, 9)):
        remote(rh.at[d, q], rh.at[d, q], csend.at[index], crecv.at[index], sib).wait_recv()

    slots = RING * group
    expert = (node * 2 + z // 2).astype(F32)
    info = rh[0, :, :, half:].reshape(slots, META).astype(F32)
    lane = lax.broadcasted_iota(jnp.int32, (slots, META), 1)
    shares = pltpu.roll(info, META - 8, 1) + pltpu.roll(info, META - 24, 1)
    factor = jnp.sum(
        jnp.where((lane < TOP) & (info == expert), shares, 0.0), axis=1, keepdims=True
    )
    s_no = lax.broadcasted_iota(jnp.int32, (slots, 1), 0)
    home = (lax.rem(s_no // CAP, RING) * block).astype(F32)
    token = jnp.where(info[:, 17:18] > 0.5, info[:, 16:17] + home, -1.0)
    for g in range(RING):
        column = jnp.broadcast_to(token[g * group : (g + 1) * group], (group, META))
        column = jnp.concatenate([column, jnp.full((META - group, META), -1.0, F32)], axis=0)
        ac[c, z, slots : slots + 16, g * META : (g + 1) * META] = column.T[:16].astype(BF16)

    loads[2].wait()
    loads[3].wait()

    def turned(v):
        pieces = [
            v[(yy * RING + xx) * CAP : (yy * RING + xx + 1) * CAP]
            for xx in range(RING)
            for yy in range(RING)
        ]
        return jnp.concatenate(pieces, axis=0)

    @pl.loop(0, wg.shape[1] // tile)
    def _(j):
        cols = pl.ds(pl.multiple_of(j * tile, tile), tile)
        one = rh[0, :, :, :half].reshape(slots, half)
        two = rh[1, :, :, :half].reshape(slots, half)
        g = dot(one, wg[:half, cols]) + turned(dot(two, wg[half:, cols]))
        u = dot(one, wu[:half, cols]) + turned(dot(two, wu[half:, cols]))
        ac[c, z, :slots, cols] = (g / (1.0 + jnp.exp(-g)) * u * factor).astype(BF16)

    arow = ac.shape[2] // 32 * 16
    gg = Gather(
        lambda q: ac.at[c, q],
        lambda q: ac.at[c, q, pl.ds(0, arow)],
        lambda q: ac.at[c, q, pl.ds(arow, ac.shape[2] - arow)],
        z,
        z_plus,
        z_minus,
        gsend,
        grecv,
        sib,
    )
    gg.start()
    gg.pass_on()
    oo[:, group:META] = jnp.zeros((RING, META - group, oo.shape[2]), BF16)
    oo[:, META + group :] = jnp.zeros((RING, META - group, oo.shape[2]), BF16)
    loads[5].wait()
    gg.finish()
    gg.shared(lambda q: ac.at[d, q])

    width = oo.shape[2]
    deep = ac.shape[3]
    for e in range(2):
        for lo in range(0, width, tile):
            hi = min(lo + tile, width)
            res = jnp.zeros((slots, hi - lo), F32)
            for zz in range(2):
                for cc in range(2):
                    k = zz * 2 + cc
                    res += dot(ac[cc, e * 2 + zz, :slots, :], wd[e, k * deep : (k + 1) * deep, lo:hi])
            for g in range(RING):
                oo[g, e * META : e * META + group, lo:hi] = res[
                    g * group : (g + 1) * group
                ].astype(BF16)
    row_no = lax.broadcasted_iota(jnp.int32, (tokens, META), 0).astype(F32)
    ht = block // 2
    for g in range(RING):
        spread = [
            jnp.where(
                ac[0, e * 2, slots : slots + 1, g * META : (g + 1) * META].astype(F32) == row_no,
                1.0,
                0.0,
            ).astype(BF16)
            for e in range(2)
        ]
        sums = dot(jnp.concatenate(spread, axis=1), oo[g]).astype(BF16)
        for q in range(RING):
            pp[0, g, q] = sums[q * block : q * block + ht]
            pp[1, q, g] = sums[q * block + ht : (q + 1) * block]

    def scatter_sum(h, held, near, full, pos, plus, minus, base):
        before, after = dn1(pos), up1(pos)
        far = up1(after)
        depth = held.shape[1] // 2
        front, back = pl.ds(0, depth), pl.ds(depth, depth)
        one = remote(held.at[far, front], near.at[0], rsend.at[base], rrecv.at[base], plus)
        two = remote(held.at[far, back], near.at[1], rsend.at[base + 1], rrecv.at[base + 1], minus)
        three = remote(held.at[after], full.at[0], rsend.at[base + 2], rrecv.at[base + 2], plus)
        four = remote(held.at[before], full.at[1], rsend.at[base + 3], rrecv.at[base + 3], minus)

        def first():
            one.start()
            two.start()

        def second():
            one.wait_recv()
            held[after, :depth] = (held[after, :depth].astype(F32) + near[0].astype(F32)).astype(BF16)
            three.start()
            two.wait_recv()
            held[before, depth:] = (
                held[before, depth:].astype(F32) + near[1].astype(F32)
            ).astype(BF16)
            four.start()

        def third():
            three.wait_recv()
            four.wait_recv()
            for copy in (one, two, three, four):
                copy.wait_send()
            return held[pos].astype(F32) + full[0].astype(F32) + full[1].astype(F32)

        return first, second, third

    axes = ((x, x_plus, x_minus), (y, y_plus, y_minus))
    steps = [
        scatter_sum(h, pp.at[h], r1.at[h], r2.at[h], *axes[h], 4 * h) for h in range(2)
    ]
    more = [
        scatter_sum(h, t1.at[h], r3.at[h], r4.at[h], *axes[1 - h], 8 + 4 * h) for h in range(2)
    ]
    for first, _, _ in steps:
        first()
    for _, second, _ in steps:
        second()
    for h in range(2):
        t1[h] = steps[h][2]().astype(BF16)
        more[h][0]()
    for _, second, _ in more:
        second()
    cols = pl.ds(pl.multiple_of(lax.rem(local, RING) * width, 128), width)
    left = zh[z // 2, :, :, cols].reshape(block, width).astype(F32)
    for h in range(2):
        kept = pl.ds(h * ht, ht)
        out[h * ht : (h + 1) * ht] = (
            left[h * ht : (h + 1) * ht] + sres[kept, :] + more[h][2]()
        ).astype(BF16)

    for gather in (zg, ag, sh, gg):
        gather.drain()
    for copy in routed:
        copy.wait_send()


def body(hid, ids, aff, gain, gate, up, down, sgate, sup, sdown):
    rows, width = hid.shape
    half = width // 2
    block = rows * 2 * RING
    units = gate.shape[2]
    cols = down.shape[2]
    shared = sgate.shape[1]
    group = RING * CAP
    slots = RING * group
    ht = block // 2
    dma = pltpu.SemaphoreType.DMA
    hbm = pl.BlockSpec(memory_space=pl.ANY)
    vmem = pl.BlockSpec(memory_space=pltpu.VMEM)
    return pl.pallas_call(
        kernel,
        out_shape=jax.ShapeDtypeStruct((block, cols), BF16),
        in_specs=[vmem] * 4 + [hbm] * 6,
        out_specs=vmem,
        scratch_shapes=[
            pltpu.VMEM((width, units), BF16),
            pltpu.VMEM((width, units), BF16),
            pltpu.VMEM(down.shape, BF16),
            pltpu.VMEM(sgate.shape, BF16),
            pltpu.VMEM(sup.shape, BF16),
            pltpu.VMEM(sdown.shape, BF16),
            pltpu.VMEM((rows, half + META), F32),
            pltpu.VMEM((rows, half + META), F32),
            pltpu.VMEM((2, RING, 2 * rows, half + META), BF16),
            pltpu.VMEM((RING, block, half + META), BF16),
            pltpu.VMEM((block, half), BF16),
            pltpu.VMEM((META, RING * block), F32),
            pltpu.VMEM((3, group, half + META), BF16),
            pltpu.VMEM((2, group // 2, half + META), BF16),
            pltpu.VMEM((2, RING, group, half + META), BF16),
            pltpu.VMEM((2, RING, slots + 16, units), BF16),
            pltpu.VMEM((2, RING, block, shared), BF16),
            pltpu.VMEM((block, cols), F32),
            pltpu.VMEM((RING, 2 * META, cols), BF16),
            pltpu.VMEM((2, RING, RING, ht, cols), BF16),
            pltpu.VMEM((2, 2, RING // 2, ht, cols), BF16),
            pltpu.VMEM((2, 2, RING, ht, cols), BF16),
            pltpu.VMEM((2, RING, ht, cols), BF16),
            pltpu.VMEM((2, 2, ht // 2, cols), BF16),
            pltpu.VMEM((2, 2, ht, cols), BF16),
            dma((6,)),
            dma((2,)),
            dma((8,)),
            dma((8,)),
            dma((4,)),
            dma((4,)),
            dma((8,)),
            dma((8,)),
            dma((10,)),
            dma((10,)),
            dma((8,)),
            dma((8,)),
            dma((16,)),
            dma((16,)),
        ],
        compiler_params=pltpu.CompilerParams(
            collective_id=0, has_side_effects=True, vmem_limit_bytes=63 * 1024 * 1024
        ),
    )(hid, ids, aff, gain.reshape(2, 1, half), gate, up, down, sgate, sup, sdown)


def solution(mesh):
    in_specs = (
        P(("node", "local"), None),
        P(("node", "local"), None),
        P(("node", "local"), None),
        P(),
        P(("node", "local"), None, None),
        P(("node", "local"), None, None),
        P("node", None, "local"),
        P(None, "local"),
        P(None, "local"),
        P(None, "local"),
    )
    return jax.shard_map(
        body, mesh=mesh, in_specs=in_specs, out_specs=P("node", "local"), check_vma=False
    )
```

```python
import functools

import jax
import jax.numpy as jnp
from jax import lax
from jax.experimental import pallas as pl
from jax.experimental.pallas import tpu as pltpu
from jax.sharding import PartitionSpec as P

MESH = pl.DeviceIdType.MESH
F32 = jnp.float32
BF16 = jnp.bfloat16
RING = 4
META = 128
CAP = 24
TOP = 8


def remote(src, dst, send, recv, device):
    return pltpu.make_async_remote_copy(
        src_ref=src,
        dst_ref=dst,
        send_sem=send,
        recv_sem=recv,
        device_id=device,
        device_id_type=MESH,
    )


def dot(a, b):
    return jnp.dot(a, b, preferred_element_type=F32)


class Gather:
    def __init__(self, slot, pos, peers, send, recv, other):
        self.slot, self.pos, self.peers, self.other = slot, pos, peers, other
        self.send, self.recv = send, recv
        self.origins = [lax.rem(pos + step, RING) for step in (3, 1, 2)]
        self.sent = []

    def copy(self, ref, index, device):
        return remote(ref, ref, self.send.at[index], self.recv.at[index], device)

    def go(self, ref, index, device):
        copy = self.copy(ref, index, device)
        copy.start()
        self.sent.append(copy)

    def start(self):
        for index, device in enumerate(self.peers):
            self.go(self.slot(self.pos), index, device)
        self.go(self.slot(self.pos), 3, self.other)

    def arrive(self):
        for index, origin in enumerate(self.origins):
            self.copy(self.slot(origin), index, self.other).wait_recv()
            self.go(self.slot(origin), 4 + index, self.other)

    def shared(self, mirror):
        for index, origin in enumerate([self.pos] + self.origins):
            self.copy(mirror(origin), 3 + index, self.other).wait_recv()

    def drain(self):
        for copy in self.sent:
            copy.wait_send()


def kernel(
    hid,
    ids,
    aff,
    gain,
    gate_hbm,
    up_hbm,
    down_hbm,
    sgate_hbm,
    sup_hbm,
    sdown_hbm,
    out,
    wg,
    wu,
    wd,
    sg,
    su,
    sd,
    pair_out,
    pair_in,
    zh,
    xa,
    xo,
    ct,
    pm,
    cs,
    rh,
    ac,
    sa,
    sres,
    oo,
    pp,
    r1,
    r2,
    t1,
    wsem,
    bsem,
    zsend,
    zrecv,
    asend,
    arecv,
    ssend,
    srecv,
    csend,
    crecv,
    gsend,
    grecv,
    rsend,
    rrecv,
):
    half = hid.shape[1] // 2
    node, local = lax.axis_index("node"), lax.axis_index("local")
    y, x = node // RING, lax.rem(node, RING)
    z, c = local // 2, lax.rem(local, 2)
    d = 1 - c
    sib = (node, z * 2 + d)
    moves = (1, 3, 2)
    step = lambda v, by: lax.rem(v + by, RING)
    z_peers = [(node, step(z, by) * 2 + c) for by in moves]
    x_peers = [(y * RING + step(x, by), local) for by in moves]
    y_peers = [(step(y, by) * RING + x, local) for by in moves]
    a_peers = [(d * v[0] + c * u[0], local) for u, v in zip(x_peers, y_peers)]
    b_peers = [(d * u[0] + c * v[0], local) for u, v in zip(x_peers, y_peers)]
    apos, bpos = d * y + c * x, d * x + c * y

    barrier = pltpu.get_barrier_semaphore()
    everyone = [sib] + z_peers + x_peers + y_peers
    for peer in everyone:
        pl.semaphore_signal(barrier, inc=1, device_id=peer, device_id_type=MESH)

    values = hid[...].astype(F32)
    scale = lax.rsqrt(jnp.mean(values * values, axis=-1, keepdims=True) + 1e-06)
    s_hi = scale.astype(BF16).astype(F32)
    s_mid = (scale - s_hi).astype(BF16).astype(F32)
    s_lo = scale - s_hi - s_mid
    weight = aff[...].astype(F32)
    mix = 2.5 * weight / jnp.sum(weight, axis=-1, keepdims=True)
    m_hi = mix.astype(BF16).astype(F32)
    m_lo = mix - m_hi
    named = ids[...].astype(F32)
    rows = hid.shape[0]
    lane = lax.broadcasted_iota(jnp.int32, (rows, META), 1)
    place = (z * 2 * rows + c * rows + lax.broadcasted_iota(jnp.int32, (rows, META), 0)).astype(F32)
    meta = jnp.where(lane == 16, place, 0.0)
    meta = jnp.where(lane == 17, 1.0, meta)
    meta = jnp.where(lane == 18, s_hi, meta)
    meta = jnp.where(lane == 19, s_mid, meta)
    meta = jnp.where(lane == 20, s_lo, meta)
    for k in range(TOP):
        meta = jnp.where(lane == k, named[:, k : k + 1], meta)
        meta = jnp.where(lane == 8 + k, m_hi[:, k : k + 1], meta)
        meta = jnp.where(lane == 24 + k, m_lo[:, k : k + 1], meta)
    other_cols = pl.ds(pl.multiple_of(d * half, 128), half)
    own_cols = pl.ds(pl.multiple_of(c * half, 128), half)
    pair_out[:, :half] = hid[:, other_cols].astype(F32)
    pair_out[:, half:] = meta

    pl.semaphore_wait(barrier, len(everyone))
    pair = remote(pair_out, pair_in, bsem.at[0], bsem.at[1], sib)
    pair.start()
    loads = [
        pltpu.make_async_copy(src, dst, wsem.at[i])
        for i, (src, dst) in enumerate(
            (
                (sgate_hbm, sg),
                (sup_hbm, su),
                (gate_hbm.at[0], wg),
                (up_hbm.at[0], wu),
                (sdown_hbm, sd),
                (down_hbm, wd),
            )
        )
    ]
    for load in loads:
        load.start()
    own = jnp.concatenate([hid[:, own_cols].astype(F32), meta], axis=1)
    pair.wait()
    theirs = pair_in[...]
    zh[c, z] = jnp.concatenate(
        [jnp.where(c == 0, own, theirs), jnp.where(c == 0, theirs, own)], axis=0
    ).astype(BF16)

    zg = Gather(lambda q: zh.at[c, q], z, z_peers, zsend, zrecv, sib)
    zg.start()
    zg.arrive()

    block = RING * zh.shape[2]

    def normed(h):
        held = zh[h].reshape(block, half + META)
        info = held[:, half:].astype(F32)
        by = info[:, 18:19] + info[:, 19:20] + info[:, 20:21]
        return (held[:, :half].astype(F32) * by * gain[h]).astype(BF16)

    xa[apos, :, :half] = normed(c)
    xa[apos, :, half:] = zh[c, :, :, half:].reshape(block, META)

    part = block // 2
    upper, lower = pl.ds(0, part), pl.ds(part, part)
    a_prev, a_next, a_far = step(apos, 3), step(apos, 1), step(apos, 2)

    def ring(place, rows, index, device):
        return remote(
            xa.at[place, rows], xa.at[place, rows], asend.at[index], arecv.at[index], device
        )

    around = [
        ring(apos, upper, 0, a_peers[0]),
        ring(apos, lower, 1, a_peers[1]),
        ring(apos, lower, 2, a_peers[0]),
        ring(apos, upper, 3, a_peers[1]),
    ]
    for copy in around:
        copy.start()
    zg.shared(lambda q: zh.at[d, q])
    xo[...] = normed(d)

    loads[0].wait()
    loads[1].wait()
    own_rows = pl.ds(pl.multiple_of(c * half, 128), half)
    other_rows = pl.ds(pl.multiple_of(d * half, 128), half)
    mine = xa[apos, :, :half]
    s_gate = dot(mine, sg[own_rows, :]) + dot(xo[...], sg[other_rows, :])
    s_up = dot(mine, su[own_rows, :]) + dot(xo[...], su[other_rows, :])
    sa[c, z] = (s_gate / (1.0 + jnp.exp(-s_gate)) * s_up).astype(BF16)
    ring(a_prev, upper, 0, a_peers[0]).wait_recv()
    around.append(ring(a_prev, upper, 4, a_peers[0]))
    around[4].start()
    ring(a_next, lower, 1, a_peers[1]).wait_recv()
    around.append(ring(a_next, lower, 5, a_peers[1]))
    around[5].start()
    sh = Gather(lambda q: sa.at[c, q], z, z_peers, ssend, srecv, sib)
    sh.start()
    ring(a_prev, lower, 2, a_peers[0]).wait_recv()
    ring(a_next, upper, 3, a_peers[1]).wait_recv()
    ring(a_far, upper, 4, a_peers[0]).wait_recv()
    ring(a_far, lower, 5, a_peers[1]).wait_recv()

    tokens = RING * block
    info = xa[:, :, half:].reshape(tokens, META).astype(F32)
    lane = lax.broadcasted_iota(jnp.int32, (tokens, META), 1).astype(F32)
    names = jnp.zeros((tokens, META), F32)
    for k in range(TOP):
        names = jnp.where(info[:, k : k + 1] == lane, 1.0, names)
    t_row = lax.broadcasted_iota(jnp.int32, (tokens, tokens), 0)
    t_col = lax.broadcasted_iota(jnp.int32, (tokens, tokens), 1)
    earlier = jnp.where((t_col < t_row) & (t_col // block == t_row // block), 1.0, 0.0)
    counts = dot(earlier.astype(BF16), names.astype(BF16))
    base = (lax.broadcasted_iota(jnp.int32, (tokens, META), 0) // (2 * block) * CAP).astype(F32)
    ct[...] = jnp.where(names > 0.5, counts + base, -1.0).T

    duo = 2 * CAP
    tile = 256
    tiles = half // tile
    slot_no = lax.broadcasted_iota(jnp.int32, (duo, tokens), 0).astype(F32)
    parity = lax.rem(lax.broadcasted_iota(jnp.int32, (duo, tokens), 1) // block, 2)
    routed = []

    def pick(group):
        chosen = []
        for by in range(RING):
            there = step(bpos, by)
            expert = (d * (y * RING + there) + c * (there * RING + x)) * 2 + z // 2
            hit = (ct[pl.ds(expert, 1), :] == slot_no) & (parity == lax.rem(bpos + group, 2))
            chosen.append(jnp.where(hit, 1.0, 0.0).astype(BF16))
        pm[...] = jnp.concatenate(chosen, axis=0)

        def put(cols, picked):
            rh[c, group, bpos, :, cols] = picked[:duo]
            for i in range(3):
                cs[group, i, :, cols] = picked[(i + 1) * duo : (i + 2) * duo]

        @pl.loop(0, tiles)
        def _(j):
            cols = pl.ds(pl.multiple_of(j * tile, tile), tile)
            put(cols, dot(pm[...], xa[:, :, cols].reshape(tokens, tile)).astype(BF16))

        put(
            pl.ds(half, META),
            dot(pm[...], xa[:, :, half:].reshape(tokens, META)).astype(BF16),
        )
        for index in (2, 0, 1):
            send(group, index).start()
        give(group, bpos, 0)

    def send(group, index):
        sem = group * 3 + index
        copy = remote(
            cs.at[group, moves[index] - 1],
            rh.at[c, group, bpos],
            csend.at[sem],
            crecv.at[sem],
            b_peers[index],
        )
        routed.append(copy)
        return copy

    def give(group, place, index):
        sem = 6 + group * 4 + index
        ref = rh.at[c, group, place]
        copy = remote(ref, ref, csend.at[sem], crecv.at[sem], sib)
        copy.start()
        routed.append(copy)

    pick(0)
    pick(1)
    sh.arrive()
    sh.shared(lambda q: sa.at[d, q])
    loads[4].wait()
    total = jnp.zeros(sres.shape, F32)
    wide = sa.shape[3]
    for zz in range(RING):
        for cc in range(2):
            total += dot(sa[cc, zz], sd[(zz * 2 + cc) * wide : (zz * 2 + cc + 1) * wide, :])
    sres[...] = total
    oo[:, :, 2 * duo : META] = jnp.zeros((2, 2, META - 2 * duo, oo.shape[3]), BF16)
    oo[:, :, META + 2 * duo :] = jnp.zeros((2, 2, META - 2 * duo, oo.shape[3]), BF16)

    def collect(group):
        for index, by in ((0, 3), (1, 1), (2, 2)):
            sem = group * 3 + index
            place = step(bpos, by)
            remote(
                cs.at[group, 0], rh.at[c, group, place], csend.at[sem], crecv.at[sem], sib
            ).wait_recv()
            give(group, place, index + 1)
        for index, by in ((0, 0), (1, 3), (2, 1), (3, 2)):
            sem = 6 + group * 4 + index
            ref = rh.at[d, group, step(apos, by)]
            remote(ref, ref, csend.at[sem], crecv.at[sem], sib).wait_recv()

    slots = RING * duo
    expert = (node * 2 + z // 2).astype(F32)

    def turned(v, group):
        pieces = []
        for xx in range(RING):
            for k in range(2):
                at = (2 * k + (xx + group) % 2) * 2 + xx // 2
                pieces.append(v[at * CAP : (at + 1) * CAP])
        return jnp.concatenate(pieces, axis=0)

    def hidden(group):
        info = rh[0, group, :, :, half:].reshape(slots, META).astype(F32)
        lane = lax.broadcasted_iota(jnp.int32, (slots, META), 1)
        shares = pltpu.roll(info, META - 8, 1) + pltpu.roll(info, META - 24, 1)
        factor = jnp.sum(
            jnp.where((lane < TOP) & (info == expert), shares, 0.0), axis=1, keepdims=True
        )
        s_no = lax.broadcasted_iota(jnp.int32, (slots, 1), 0)
        home = (lax.rem(s_no // CAP, RING) * block).astype(F32)
        token = jnp.where(info[:, 17:18] > 0.5, info[:, 16:17] + home, -1.0)
        for i in range(2):
            column = jnp.broadcast_to(token[i * 2 * duo : (i + 1) * 2 * duo], (2 * duo, META))
            column = jnp.concatenate(
                [column, jnp.full((META - 2 * duo, META), -1.0, F32)], axis=0
            )
            ac[c, z, group, slots:, i * META : (i + 1) * META] = column.T[:16].astype(BF16)
        ac[c, z, group, slots:, 2 * META :] = jnp.zeros((16, ac.shape[4] - 2 * META), BF16)

        @pl.loop(0, wg.shape[1] // tile)
        def _(j):
            cols = pl.ds(pl.multiple_of(j * tile, tile), tile)
            one = rh[0, group, :, :, :half].reshape(slots, half)
            two = rh[1, group, :, :, :half].reshape(slots, half)
            g = dot(one, wg[:half, cols]) + turned(dot(two, wg[half:, cols]), group)
            u = dot(one, wu[:half, cols]) + turned(dot(two, wu[half:, cols]), group)
            ac[c, z, group, :slots, cols] = (g / (1.0 + jnp.exp(-g)) * u * factor).astype(BF16)

        return Gather(
            lambda q: ac.at[c, q, group], z, z_peers, gsend.at[group], grecv.at[group], sib
        )

    collect(0)
    loads[2].wait()
    loads[3].wait()
    gg = [hidden(0)]
    gg[0].start()
    collect(1)
    gg.append(hidden(1))
    gg[1].start()

    width = oo.shape[3]
    deep = ac.shape[4]
    ht = block // 2
    row_no = lax.broadcasted_iota(jnp.int32, (tokens, META), 0).astype(F32)

    def outputs(group):
        for e in range(2):
            for lo in range(0, width, tile):
                hi = min(lo + tile, width)
                res = jnp.zeros((slots, hi - lo), F32)
                for zz in range(2):
                    for cc in range(2):
                        k = zz * 2 + cc
                        res += dot(
                            ac[cc, e * 2 + zz, group, :slots, :],
                            wd[e, k * deep : (k + 1) * deep, lo:hi],
                        )
                for i in range(2):
                    oo[group, i, e * META : e * META + 2 * duo, lo:hi] = res[
                        i * 2 * duo : (i + 1) * 2 * duo
                    ].astype(BF16)
        for i in range(2):
            spread = [
                jnp.where(
                    ac[0, e * 2, group, slots : slots + 1, i * META : (i + 1) * META].astype(F32)
                    == row_no,
                    1.0,
                    0.0,
                ).astype(BF16)
                for e in range(2)
            ]
            sums = dot(jnp.concatenate(spread, axis=1), oo[group, i]).astype(BF16)
            for p in range(2):
                for k in range(2):
                    xx = i * 2 + p
                    yy = 2 * k + (xx + group) % 2
                    at = (p * 2 + k) * block
                    pp[0, group, xx, k] = sums[at : at + ht]
                    pp[1, group, yy, i] = sums[at + ht : at + block]

    axes = ((x, x_peers), (y, y_peers))
    sums1, sums2 = [], []

    def spread_first(group):
        for h in range(2):
            pos, peers = axes[h]
            for index, by in enumerate(moves):
                sem = (group * 2 + h) * 3 + index
                copy = remote(
                    pp.at[h, group, step(pos, by)],
                    r1.at[h, group, index],
                    rsend.at[sem],
                    rrecv.at[sem],
                    peers[index],
                )
                copy.start()
                sums1.append(copy)

    def sum_first(group):
        for h in range(2):
            pos = axes[h][0]
            for index in range(3):
                sums1[(group * 2 + h) * 3 + index].wait_recv()
            whole = pp[h, group, pos].astype(F32)
            for index in range(3):
                whole += r1[h, group, index].astype(F32)
            for k in range(2):
                t1[h, 2 * k + lax.rem(pos + group, 2)] = whole[k].astype(BF16)

    gg[0].arrive()
    gg[0].shared(lambda q: ac.at[d, q, 0])
    loads[5].wait()
    outputs(0)
    spread_first(0)
    gg[1].arrive()
    gg[1].shared(lambda q: ac.at[d, q, 1])
    outputs(1)
    spread_first(1)
    sum_first(0)
    sum_first(1)
    for h in range(2):
        pos, peers = axes[1 - h]
        for index, by in enumerate(moves):
            sem = 12 + h * 3 + index
            copy = remote(
                t1.at[h, step(pos, by)],
                r2.at[h, index],
                rsend.at[sem],
                rrecv.at[sem],
                peers[index],
            )
            copy.start()
            sums2.append(copy)
    cols = pl.ds(pl.multiple_of(lax.rem(local, RING) * width, 128), width)
    left = zh[z // 2, :, :, cols].reshape(block, width).astype(F32) + sres[...]
    for h in range(2):
        pos = axes[1 - h][0]
        whole = left[h * ht : (h + 1) * ht] + t1[h, pos].astype(F32)
        for index in range(3):
            sums2[h * 3 + index].wait_recv()
            whole += r2[h, index].astype(F32)
        out[h * ht : (h + 1) * ht] = whole.astype(BF16)

    for gather in [zg, sh] + gg:
        gather.drain()
    for copy in around + routed + sums1 + sums2:
        copy.wait_send()


def body(hid, ids, aff, gain, gate, up, down, sgate, sup, sdown):
    rows, width = hid.shape
    half = width // 2
    block = rows * 2 * RING
    units = gate.shape[2]
    cols = down.shape[2]
    shared = sgate.shape[1]
    duo = 2 * CAP
    slots = RING * duo
    ht = block // 2
    dma = pltpu.SemaphoreType.DMA
    hbm = pl.BlockSpec(memory_space=pl.ANY)
    vmem = pl.BlockSpec(memory_space=pltpu.VMEM)
    return pl.pallas_call(
        kernel,
        out_shape=jax.ShapeDtypeStruct((block, cols), BF16),
        in_specs=[vmem] * 4 + [hbm] * 6,
        out_specs=vmem,
        scratch_shapes=[
            pltpu.VMEM((width, units), BF16),
            pltpu.VMEM((width, units), BF16),
            pltpu.VMEM(down.shape, BF16),
            pltpu.VMEM(sgate.shape, BF16),
            pltpu.VMEM(sup.shape, BF16),
            pltpu.VMEM(sdown.shape, BF16),
            pltpu.VMEM((rows, half + META), F32),
            pltpu.VMEM((rows, half + META), F32),
            pltpu.VMEM((2, RING, 2 * rows, half + META), BF16),
            pltpu.VMEM((RING, block, half + META), BF16),
            pltpu.VMEM((block, half), BF16),
            pltpu.VMEM((META, RING * block), F32),
            pltpu.VMEM((slots, RING * block), BF16),
            pltpu.VMEM((2, 3, duo, half + META), BF16),
            pltpu.VMEM((2, 2, RING, duo, half + META), BF16),
            pltpu.VMEM((2, RING, 2, slots + 16, units), BF16),
            pltpu.VMEM((2, RING, block, shared), BF16),
            pltpu.VMEM((block, cols), F32),
            pltpu.VMEM((2, 2, 2 * META, cols), BF16),
            pltpu.VMEM((2, 2, RING, 2, ht, cols), BF16),
            pltpu.VMEM((2, 2, 3, 2, ht, cols), BF16),
            pltpu.VMEM((2, 3, ht, cols), BF16),
            pltpu.VMEM((2, RING, ht, cols), BF16),
            dma((6,)),
            dma((2,)),
            dma((7,)),
            dma((7,)),
            dma((6,)),
            dma((6,)),
            dma((7,)),
            dma((7,)),
            dma((14,)),
            dma((14,)),
            dma((2, 7)),
            dma((2, 7)),
            dma((18,)),
            dma((18,)),
        ],
        compiler_params=pltpu.CompilerParams(
            collective_id=0, has_side_effects=True, vmem_limit_bytes=63 * 1024 * 1024
        ),
    )(hid, ids, aff, gain.reshape(2, 1, half), gate, up, down, sgate, sup, sdown)


def solution(mesh):
    in_specs = (
        P(("node", "local"), None),
        P(("node", "local"), None),
        P(("node", "local"), None),
        P(),
        P(("node", "local"), None, None),
        P(("node", "local"), None, None),
        P("node", None, "local"),
        P(None, "local"),
        P(None, "local"),
        P(None, "local"),
    )
    return jax.shard_map(
        body, mesh=mesh, in_specs=in_specs, out_specs=P("node", "local"), check_vma=False
    )
```

```python
import functools

import jax
import jax.numpy as jnp
from jax import lax
from jax.experimental import pallas as pl
from jax.experimental.pallas import tpu as pltpu
from jax.sharding import PartitionSpec as P

MESH = pl.DeviceIdType.MESH
F32 = jnp.float32
BF16 = jnp.bfloat16
RING = 4
META = 128
CAP = 24
TOP = 8


def remote(src, dst, send, recv, device):
    return pltpu.make_async_remote_copy(
        src_ref=src,
        dst_ref=dst,
        send_sem=send,
        recv_sem=recv,
        device_id=device,
        device_id_type=MESH,
    )


def dot(a, b):
    return jnp.dot(a, b, preferred_element_type=F32)


class Gather:
    def __init__(self, slot, pos, peers, send, recv, other):
        self.slot, self.pos, self.peers, self.other = slot, pos, peers, other
        self.send, self.recv = send, recv
        self.origins = [lax.rem(pos + step, RING) for step in (3, 1, 2)]
        self.sent = []

    def copy(self, ref, index, device):
        return remote(ref, ref, self.send.at[index], self.recv.at[index], device)

    def go(self, ref, index, device):
        copy = self.copy(ref, index, device)
        copy.start()
        self.sent.append(copy)

    def start(self):
        for index, device in enumerate(self.peers):
            self.go(self.slot(self.pos), index, device)
        self.go(self.slot(self.pos), 3, self.other)

    def arrive(self):
        for index, origin in enumerate(self.origins):
            self.copy(self.slot(origin), index, self.other).wait_recv()
            self.go(self.slot(origin), 4 + index, self.other)

    def shared(self, mirror):
        for index, origin in enumerate([self.pos] + self.origins):
            self.copy(mirror(origin), 3 + index, self.other).wait_recv()

    def drain(self):
        for copy in self.sent:
            copy.wait_send()


def kernel(
    hid,
    ids,
    aff,
    gain,
    gate_hbm,
    up_hbm,
    down_hbm,
    sgate_hbm,
    sup_hbm,
    sdown_hbm,
    out,
    wg,
    wu,
    wd,
    sg,
    su,
    sd,
    pa,
    pb,
    za,
    zb,
    xa,
    xo,
    ct,
    pm,
    cs,
    rh,
    ac,
    sa,
    sres,
    oo,
    pp,
    r1,
    r2,
    t1,
    wsem,
    zsend,
    zrecv,
    asend,
    arecv,
    ssend,
    srecv,
    csend,
    crecv,
    gsend,
    grecv,
    rsend,
    rrecv,
):
    half = hid.shape[1] // 2
    node, local = lax.axis_index("node"), lax.axis_index("local")
    y, x = node // RING, lax.rem(node, RING)
    z, c = local // 2, lax.rem(local, 2)
    d = 1 - c
    sib = (node, z * 2 + d)
    moves = (1, 3, 2)
    step = lambda v, by: lax.rem(v + by, RING)
    z_peers = [(node, step(z, by) * 2 + c) for by in moves]
    x_peers = [(y * RING + step(x, by), local) for by in moves]
    y_peers = [(step(y, by) * RING + x, local) for by in moves]
    z_cross = [(node, step(z, by) * 2 + d) for by in moves]
    a_peers = [(d * v[0] + c * u[0], local) for u, v in zip(x_peers, y_peers)]
    b_peers = [(d * u[0] + c * v[0], local) for u, v in zip(x_peers, y_peers)]
    apos, bpos = d * y + c * x, d * x + c * y

    barrier = pltpu.get_barrier_semaphore()
    everyone = [sib] + z_peers + z_cross + x_peers + y_peers
    for peer in everyone:
        pl.semaphore_signal(barrier, inc=1, device_id=peer, device_id_type=MESH)

    values = hid[...].astype(F32)
    scale = lax.rsqrt(jnp.mean(values * values, axis=-1, keepdims=True) + 1e-06)
    s_hi = scale.astype(BF16).astype(F32)
    s_mid = (scale - s_hi).astype(BF16).astype(F32)
    s_lo = scale - s_hi - s_mid
    weight = aff[...].astype(F32)
    mix = 2.5 * weight / jnp.sum(weight, axis=-1, keepdims=True)
    m_hi = mix.astype(BF16).astype(F32)
    m_lo = mix - m_hi
    named = ids[...].astype(F32)
    rows = hid.shape[0]
    lane = lax.broadcasted_iota(jnp.int32, (rows, META), 1)
    place = (z * 2 * rows + c * rows + lax.broadcasted_iota(jnp.int32, (rows, META), 0)).astype(F32)
    meta = jnp.where(lane == 16, place, 0.0)
    meta = jnp.where(lane == 17, 1.0, meta)
    meta = jnp.where(lane == 18, s_hi, meta)
    meta = jnp.where(lane == 19, s_mid, meta)
    meta = jnp.where(lane == 20, s_lo, meta)
    for k in range(TOP):
        meta = jnp.where(lane == k, named[:, k : k + 1], meta)
        meta = jnp.where(lane == 8 + k, m_hi[:, k : k + 1], meta)
        meta = jnp.where(lane == 24 + k, m_lo[:, k : k + 1], meta)
    quarter = half // 2
    eighth = quarter // 2

    def laid(h, start):
        cols = lambda i: pl.ds(pl.multiple_of(h * half + start + i * eighth, 128), eighth)
        return jnp.concatenate([hid[:, cols(i)].astype(F32) for i in range(2)], axis=0)

    beside = jnp.concatenate([meta, jnp.zeros((rows, META), F32)], axis=0).astype(BF16)
    za[c, local, :, :eighth] = laid(c, quarter).astype(BF16)
    za[c, local, :, eighth:] = beside
    zb[c, local] = laid(c, 0).astype(BF16)
    pa[:, :eighth] = laid(d, quarter).astype(BF16)
    pa[:, eighth:] = beside
    pb[...] = laid(d, 0).astype(BF16)
    pl.semaphore_wait(barrier, len(everyone))
    first = []
    for part, (mine, other, held) in enumerate(((za.at[c, local], pa, za), (zb.at[c, local], pb, zb))):
        for index, device in enumerate(z_peers + z_cross + [sib]):
            whose = c if index < 3 else d
            sem = part * 7 + index
            copy = remote(
                mine if index < 3 else other,
                held.at[whose, local],
                zsend.at[sem],
                zrecv.at[sem],
                device,
            )
            copy.start()
            first.append(copy)
    loads = [
        pltpu.make_async_copy(src, dst, wsem.at[i])
        for i, (src, dst) in enumerate(
            (
                (sgate_hbm, sg),
                (sup_hbm, su),
                (gate_hbm.at[0], wg),
                (up_hbm.at[0], wu),
                (sdown_hbm, sd),
                (down_hbm, wd),
            )
        )
    ]
    for load in loads:
        load.start()

    def gathered(part):
        held = (za, zb)[part]
        back = (3, 1, 2)
        origins = [step(z, by) * 2 + c for by in back] + [step(z, by) * 2 + d for by in back]
        origins.append(z * 2 + d)
        for index, origin in enumerate(origins):
            sem = part * 7 + index
            ref = held.at[c, origin]
            remote(ref, ref, zsend.at[sem], zrecv.at[sem], sib).wait_recv()
        copy = remote(held.at[c], held.at[c], zsend.at[14 + part], zrecv.at[14 + part], sib)
        first.append(copy)
        return copy

    block = RING * 2 * rows
    ahead = pl.ds(quarter, quarter + META)
    behind = pl.ds(0, quarter)

    def spread_out(held):
        v = held.astype(F32).reshape(2 * RING, 2, rows, held.shape[2])
        return [v[:, i].reshape(block, held.shape[2]) for i in range(2)]

    def normed(h, part):
        lead, rest = spread_out((za, zb)[part][h])
        info = spread_out(za[h, :, :, eighth:])[0]
        by = info[:, 18:19] + info[:, 19:20] + info[:, 20:21]
        start = (quarter, 0)[part]
        lead = lead[:, :eighth] * by * gain[h, :, start : start + eighth]
        rest = rest[:, :eighth] * by * gain[h, :, start + eighth : start + quarter]
        return jnp.concatenate([lead, rest], axis=1).astype(BF16)

    part_rows = block // 2
    upper, lower = pl.ds(0, part_rows), pl.ds(part_rows, part_rows)
    a_prev, a_next, a_far = step(apos, 3), step(apos, 1), step(apos, 2)

    def ring(part, place, rows_of, index, device):
        ref = xa.at[place, rows_of, (ahead, behind)[part]]
        sem = part * 6 + index
        return remote(ref, ref, asend.at[sem], arecv.at[sem], device)

    around = []

    def go(copy):
        copy.start()
        around.append(copy)

    def ring_start(part):
        go(ring(part, apos, upper, 0, a_peers[0]))
        go(ring(part, apos, lower, 1, a_peers[1]))
        go(ring(part, apos, lower, 2, a_peers[0]))
        go(ring(part, apos, upper, 3, a_peers[1]))

    def ring_on(part):
        ring(part, a_prev, upper, 0, a_peers[0]).wait_recv()
        go(ring(part, a_prev, upper, 4, a_peers[0]))
        ring(part, a_next, lower, 1, a_peers[1]).wait_recv()
        go(ring(part, a_next, lower, 5, a_peers[1]))

    def ring_end(part):
        ring(part, a_prev, lower, 2, a_peers[0]).wait_recv()
        ring(part, a_next, upper, 3, a_peers[1]).wait_recv()
        ring(part, a_far, upper, 4, a_peers[0]).wait_recv()
        ring(part, a_far, lower, 5, a_peers[1]).wait_recv()

    share = gathered(0)
    xa[apos, :, quarter:half] = normed(c, 0)
    xa[apos, :, half:] = spread_out(za[c, :, :, eighth:])[0].astype(BF16)
    ring_start(0)
    share.start()
    share = gathered(1)
    xa[apos, :, :quarter] = normed(c, 1)
    ring_start(1)
    share.start()
    ring_on(0)
    ring_on(1)
    ring_end(0)

    tokens = RING * block
    info = xa[:, :, half:].reshape(tokens, META).astype(F32)
    lane = lax.broadcasted_iota(jnp.int32, (tokens, META), 1).astype(F32)
    names = jnp.zeros((tokens, META), F32)
    for k in range(TOP):
        names = jnp.where(info[:, k : k + 1] == lane, 1.0, names)
    t_row = lax.broadcasted_iota(jnp.int32, (tokens, tokens), 0)
    t_col = lax.broadcasted_iota(jnp.int32, (tokens, tokens), 1)
    earlier = jnp.where((t_col < t_row) & (t_col // block == t_row // block), 1.0, 0.0)
    counts = dot(earlier.astype(BF16), names.astype(BF16))
    base = (lax.broadcasted_iota(jnp.int32, (tokens, META), 0) // (2 * block) * CAP).astype(F32)
    ct[...] = jnp.where(names > 0.5, counts + base, -1.0).T

    duo = 2 * CAP
    tile = 256
    tiles = quarter // tile
    slot_no = lax.broadcasted_iota(jnp.int32, (duo, tokens), 0).astype(F32)
    parity = lax.rem(lax.broadcasted_iota(jnp.int32, (duo, tokens), 1) // block, 2)
    routed = []

    def choose(group):
        for by in range(RING):
            there = step(bpos, by)
            expert = (d * (y * RING + there) + c * (there * RING + x)) * 2 + z // 2
            hit = (ct[pl.ds(expert, 1), :] == slot_no) & (parity == lax.rem(bpos + group, 2))
            pm[group, by * duo : (by + 1) * duo] = jnp.where(hit, 1.0, 0.0).astype(BF16)

    def pick(group, part):
        def put(cols, width):
            seen = xa[:, :, cols].reshape(tokens, width)
            picked = dot(pm[group], seen).astype(BF16)
            rh[c, group, bpos, :, cols] = picked[:duo]
            for i in range(3):
                cs[group, i, :, cols] = picked[(i + 1) * duo : (i + 2) * duo]

        start = (quarter, 0)[part]

        for j in range(tiles):
            put(pl.ds(start + j * tile, tile), tile)
        if part == 0:
            put(pl.ds(half, META), META)
        for index in (2, 0, 1):
            send(group, index, part).start()

    def send(group, index, part):
        sem = (group * 2 + part) * 3 + index
        cols = (ahead, behind)[part]
        copy = remote(
            cs.at[group, moves[index] - 1, :, cols],
            rh.at[c, group, bpos, :, cols],
            csend.at[sem],
            crecv.at[sem],
            b_peers[index],
        )
        routed.append(copy)
        return copy

    def give(group, place, index):
        sem = 12 + group * 4 + index
        ref = rh.at[c, group, place]
        copy = remote(ref, ref, csend.at[sem], crecv.at[sem], sib)
        copy.start()
        routed.append(copy)

    choose(0)
    pick(0, 0)
    choose(1)
    ring_end(1)
    pick(0, 1)
    give(0, bpos, 0)
    pick(1, 0)
    pick(1, 1)
    give(1, bpos, 0)
    for part, held in enumerate((za, zb)):
        ref = held.at[d]
        remote(ref, ref, zsend.at[14 + part], zrecv.at[14 + part], sib).wait_recv()
    xo[:, quarter:] = normed(d, 0)
    xo[:, :quarter] = normed(d, 1)

    loads[0].wait()
    loads[1].wait()
    own_rows = pl.ds(pl.multiple_of(c * half, 128), half)
    other_rows = pl.ds(pl.multiple_of(d * half, 128), half)
    mine = xa[apos, :, :half]
    s_gate = dot(mine, sg[own_rows, :]) + dot(xo[...], sg[other_rows, :])
    s_up = dot(mine, su[own_rows, :]) + dot(xo[...], su[other_rows, :])
    sa[c, z] = (s_gate / (1.0 + jnp.exp(-s_gate)) * s_up).astype(BF16)
    sh = Gather(lambda q: sa.at[c, q], z, z_peers, ssend, srecv, sib)
    sh.start()
    oo[:, :, 2 * duo : META] = jnp.zeros((2, 2, META - 2 * duo, oo.shape[3]), BF16)
    oo[:, :, META + 2 * duo :] = jnp.zeros((2, 2, META - 2 * duo, oo.shape[3]), BF16)

    def collect(group):
        for index, by in ((0, 3), (1, 1), (2, 2)):
            place = step(bpos, by)
            for part in range(2):
                sem = (group * 2 + part) * 3 + index
                ref = rh.at[c, group, place, :, (ahead, behind)[part]]
                remote(ref, ref, csend.at[sem], crecv.at[sem], sib).wait_recv()
            give(group, place, index + 1)
        for index, by in ((0, 0), (1, 3), (2, 1), (3, 2)):
            sem = 12 + group * 4 + index
            ref = rh.at[d, group, step(apos, by)]
            remote(ref, ref, csend.at[sem], crecv.at[sem], sib).wait_recv()

    slots = RING * duo
    expert = (node * 2 + z // 2).astype(F32)

    def turned(v, group):
        pieces = []
        for xx in range(RING):
            for k in range(2):
                at = (2 * k + (xx + group) % 2) * 2 + xx // 2
                pieces.append(v[at * CAP : (at + 1) * CAP])
        return jnp.concatenate(pieces, axis=0)

    def hidden(group):
        info = rh[0, group, :, :, half:].reshape(slots, META).astype(F32)
        lane = lax.broadcasted_iota(jnp.int32, (slots, META), 1)
        shares = pltpu.roll(info, META - 8, 1) + pltpu.roll(info, META - 24, 1)
        factor = jnp.sum(
            jnp.where((lane < TOP) & (info == expert), shares, 0.0), axis=1, keepdims=True
        )
        s_no = lax.broadcasted_iota(jnp.int32, (slots, 1), 0)
        home = (lax.rem(s_no // CAP, RING) * block).astype(F32)
        token = jnp.where(info[:, 17:18] > 0.5, info[:, 16:17] + home, -1.0)
        for i in range(2):
            column = jnp.broadcast_to(token[i * 2 * duo : (i + 1) * 2 * duo], (2 * duo, META))
            column = jnp.concatenate(
                [column, jnp.full((META - 2 * duo, META), -1.0, F32)], axis=0
            )
            ac[c, z, group, slots:, i * META : (i + 1) * META] = column.T[:16].astype(BF16)
        ac[c, z, group, slots:, 2 * META :] = jnp.zeros((16, ac.shape[4] - 2 * META), BF16)

        gathers = []
        for j in range(wg.shape[1] // tile):
            cols = pl.ds(j * tile, tile)
            one = rh[0, group, :, :, :half].reshape(slots, half)
            two = rh[1, group, :, :, :half].reshape(slots, half)
            g = dot(one, wg[:half, cols]) + turned(dot(two, wg[half:, cols]), group)
            u = dot(one, wu[:half, cols]) + turned(dot(two, wu[half:, cols]), group)
            ac[c, z, group, :slots, cols] = (g / (1.0 + jnp.exp(-g)) * u * factor).astype(BF16)
            gather = Gather(
                lambda q, cols=cols: ac.at[c, q, group, :, cols],
                z,
                z_peers,
                gsend.at[group, j],
                grecv.at[group, j],
                sib,
            )
            gather.start()
            gathers.append(gather)
        return gathers

    def hidden_in(group):
        for gather in gg[group]:
            gather.arrive()
        for j, gather in enumerate(gg[group]):
            gather.shared(lambda q: ac.at[d, q, group, :, pl.ds(j * tile, tile)])

    collect(0)
    loads[2].wait()
    loads[3].wait()
    gg = [hidden(0)]
    collect(1)
    gg.append(hidden(1))
    sh.arrive()
    sh.shared(lambda q: sa.at[d, q])
    loads[4].wait()
    total = jnp.zeros(sres.shape, F32)
    wide = sa.shape[3]
    for zz in range(RING):
        for cc in range(2):
            total += dot(sa[cc, zz], sd[(zz * 2 + cc) * wide : (zz * 2 + cc + 1) * wide, :])
    sres[...] = total

    width = oo.shape[3]
    deep = ac.shape[4]
    ht = block // 2
    row_no = lax.broadcasted_iota(jnp.int32, (tokens, META), 0).astype(F32)

    def outputs(group):
        for e in range(2):
            for lo in range(0, width, tile):
                hi = min(lo + tile, width)
                res = jnp.zeros((slots, hi - lo), F32)
                for zz in range(2):
                    for cc in range(2):
                        k = zz * 2 + cc
                        res += dot(
                            ac[cc, e * 2 + zz, group, :slots, :],
                            wd[e, k * deep : (k + 1) * deep, lo:hi],
                        )
                for i in range(2):
                    oo[group, i, e * META : e * META + 2 * duo, lo:hi] = res[
                        i * 2 * duo : (i + 1) * 2 * duo
                    ].astype(BF16)
        for i in range(2):
            spread = [
                jnp.where(
                    ac[0, e * 2, group, slots : slots + 1, i * META : (i + 1) * META].astype(F32)
                    == row_no,
                    1.0,
                    0.0,
                ).astype(BF16)
                for e in range(2)
            ]
            sums = dot(jnp.concatenate(spread, axis=1), oo[group, i]).astype(BF16)
            for p in range(2):
                for k in range(2):
                    xx = i * 2 + p
                    yy = 2 * k + (xx + group) % 2
                    at = (p * 2 + k) * block
                    pp[0, group, xx, k] = sums[at : at + ht]
                    pp[1, group, yy, i] = sums[at + ht : at + block]

    axes = ((x, x_peers), (y, y_peers))
    sums1, sums2 = [], []

    def spread_first(group):
        for h in range(2):
            pos, peers = axes[h]
            for index, by in enumerate(moves):
                sem = (group * 2 + h) * 3 + index
                copy = remote(
                    pp.at[h, group, step(pos, by)],
                    r1.at[h, group, index],
                    rsend.at[sem],
                    rrecv.at[sem],
                    peers[index],
                )
                copy.start()
                sums1.append(copy)

    def sum_first(group):
        for h in range(2):
            pos = axes[h][0]
            for index in range(3):
                sums1[(group * 2 + h) * 3 + index].wait_recv()
            whole = pp[h, group, pos].astype(F32)
            for index in range(3):
                whole += r1[h, group, index].astype(F32)
            for k in range(2):
                t1[h, 2 * k + lax.rem(pos + group, 2)] = whole[k].astype(BF16)

    hidden_in(0)
    loads[5].wait()
    outputs(0)
    spread_first(0)
    hidden_in(1)
    outputs(1)
    spread_first(1)
    sum_first(0)
    sum_first(1)
    for h in range(2):
        pos, peers = axes[1 - h]
        for index, by in enumerate(moves):
            sem = 12 + h * 3 + index
            copy = remote(
                t1.at[h, step(pos, by)],
                r2.at[h, index],
                rsend.at[sem],
                rrecv.at[sem],
                peers[index],
            )
            copy.start()
            sums2.append(copy)
    fore = spread_out(za[z // 2, :, :, :eighth])
    aft = spread_out(zb[z // 2])
    late = lax.rem(z, 2) == 1
    left = jnp.where(
        late,
        jnp.where(c == 0, fore[0], fore[1]),
        jnp.where(c == 0, aft[0], aft[1]),
    )
    left = left + sres[...]
    for h in range(2):
        pos = axes[1 - h][0]
        whole = left[h * ht : (h + 1) * ht] + t1[h, pos].astype(F32)
        for index in range(3):
            sums2[h * 3 + index].wait_recv()
            whole += r2[h, index].astype(F32)
        out[h * ht : (h + 1) * ht] = whole.astype(BF16)

    for gather in [sh] + gg[0] + gg[1]:
        gather.drain()
    for copy in first + around + routed + sums1 + sums2:
        copy.wait_send()


def body(hid, ids, aff, gain, gate, up, down, sgate, sup, sdown):
    rows, width = hid.shape
    half = width // 2
    block = rows * 2 * RING
    units = gate.shape[2]
    cols = down.shape[2]
    shared = sgate.shape[1]
    duo = 2 * CAP
    slots = RING * duo
    ht = block // 2
    dma = pltpu.SemaphoreType.DMA
    hbm = pl.BlockSpec(memory_space=pl.ANY)
    vmem = pl.BlockSpec(memory_space=pltpu.VMEM)
    return pl.pallas_call(
        kernel,
        out_shape=jax.ShapeDtypeStruct((block, cols), BF16),
        in_specs=[vmem] * 4 + [hbm] * 6,
        out_specs=vmem,
        scratch_shapes=[
            pltpu.VMEM((width, units), BF16),
            pltpu.VMEM((width, units), BF16),
            pltpu.VMEM(down.shape, BF16),
            pltpu.VMEM(sgate.shape, BF16),
            pltpu.VMEM(sup.shape, BF16),
            pltpu.VMEM(sdown.shape, BF16),
            pltpu.VMEM((2 * rows, half // 4 + META), BF16),
            pltpu.VMEM((2 * rows, half // 4), BF16),
            pltpu.VMEM((2, 2 * RING, 2 * rows, half // 4 + META), BF16),
            pltpu.VMEM((2, 2 * RING, 2 * rows, half // 4), BF16),
            pltpu.VMEM((RING, block, half + META), BF16),
            pltpu.VMEM((block, half), BF16),
            pltpu.VMEM((META, RING * block), F32),
            pltpu.VMEM((2, slots, RING * block), BF16),
            pltpu.VMEM((2, 3, duo, half + META), BF16),
            pltpu.VMEM((2, 2, RING, duo, half + META), BF16),
            pltpu.VMEM((2, RING, 2, slots + 16, units), BF16),
            pltpu.VMEM((2, RING, block, shared), BF16),
            pltpu.VMEM((block, cols), F32),
            pltpu.VMEM((2, 2, 2 * META, cols), BF16),
            pltpu.VMEM((2, 2, RING, 2, ht, cols), BF16),
            pltpu.VMEM((2, 2, 3, 2, ht, cols), BF16),
            pltpu.VMEM((2, 3, ht, cols), BF16),
            pltpu.VMEM((2, RING, ht, cols), BF16),
            dma((6,)),
            dma((16,)),
            dma((16,)),
            dma((12,)),
            dma((12,)),
            dma((7,)),
            dma((7,)),
            dma((20,)),
            dma((20,)),
            dma((2, 2, 7)),
            dma((2, 2, 7)),
            dma((18,)),
            dma((18,)),
        ],
        compiler_params=pltpu.CompilerParams(
            collective_id=0, has_side_effects=True, vmem_limit_bytes=63 * 1024 * 1024
        ),
    )(hid, ids, aff, gain.reshape(2, 1, half), gate, up, down, sgate, sup, sdown)


def solution(mesh):
    in_specs = (
        P(("node", "local"), None),
        P(("node", "local"), None),
        P(("node", "local"), None),
        P(),
        P(("node", "local"), None, None),
        P(("node", "local"), None, None),
        P("node", None, "local"),
        P(None, "local"),
        P(None, "local"),
        P(None, "local"),
    )
    return jax.shard_map(
        body, mesh=mesh, in_specs=in_specs, out_specs=P("node", "local"), check_vma=False
    )
```

```python
import functools

import jax
import jax.numpy as jnp
from jax import lax
from jax.experimental import pallas as pl
from jax.experimental.pallas import tpu as pltpu
from jax.sharding import PartitionSpec as P

MESH = pl.DeviceIdType.MESH
F32 = jnp.float32
BF16 = jnp.bfloat16
RING = 4
META = 128
CAP = 24
TOP = 8


def remote(src, dst, send, recv, device):
    return pltpu.make_async_remote_copy(
        src_ref=src,
        dst_ref=dst,
        send_sem=send,
        recv_sem=recv,
        device_id=device,
        device_id_type=MESH,
    )


def dot(a, b):
    return jnp.dot(a, b, preferred_element_type=F32)


class Gather:
    def __init__(self, slot, pos, peers, send, recv, other):
        self.slot, self.pos, self.peers, self.other = slot, pos, peers, other
        self.send, self.recv = send, recv
        self.origins = [lax.rem(pos + step, RING) for step in (3, 1, 2)]
        self.sent = []

    def copy(self, ref, index, device):
        return remote(ref, ref, self.send.at[index], self.recv.at[index], device)

    def go(self, ref, index, device):
        copy = self.copy(ref, index, device)
        copy.start()
        self.sent.append(copy)

    def start(self):
        for index, device in enumerate(self.peers):
            self.go(self.slot(self.pos), index, device)
        self.go(self.slot(self.pos), 3, self.other)

    def arrive(self):
        for index, origin in enumerate(self.origins):
            self.copy(self.slot(origin), index, self.other).wait_recv()
            self.go(self.slot(origin), 4 + index, self.other)

    def shared(self, mirror):
        for index, origin in enumerate([self.pos] + self.origins):
            self.copy(mirror(origin), 3 + index, self.other).wait_recv()

    def settle(self):
        for copy in self.sent[:3]:
            copy.wait_send()
        self.sent = self.sent[3:]

    def drain(self):
        for copy in self.sent:
            copy.wait_send()


def kernel(
    hid_hbm,
    ids_hbm,
    aff_hbm,
    gain_hbm,
    gate_hbm,
    up_hbm,
    down_hbm,
    sgate_hbm,
    sup_hbm,
    sdown_hbm,
    out,
    hid,
    ids,
    aff,
    gain,
    wg,
    wu,
    wd,
    sg,
    su,
    sd,
    pa,
    pb,
    za,
    zb,
    xa,
    xo,
    ct,
    pm,
    cs,
    rh,
    ac,
    sa,
    sres,
    acc,
    oo,
    pp,
    r1,
    r2,
    t1,
    wsem,
    zsend,
    zrecv,
    asend,
    arecv,
    ssend,
    srecv,
    csend,
    crecv,
    gsend,
    grecv,
    rsend,
    rrecv,
):
    half = hid.shape[1] // 2
    node, local = lax.axis_index("node"), lax.axis_index("local")
    y, x = node // RING, lax.rem(node, RING)
    z, c = local // 2, lax.rem(local, 2)
    d = 1 - c
    sib = (node, z * 2 + d)
    moves = (1, 3, 2)
    step = lambda v, by: lax.rem(v + by, RING)
    z_peers = [(node, step(z, by) * 2 + c) for by in moves]
    x_peers = [(y * RING + step(x, by), local) for by in moves]
    y_peers = [(step(y, by) * RING + x, local) for by in moves]
    z_cross = [(node, step(z, by) * 2 + d) for by in moves]
    a_peers = [(d * v[0] + c * u[0], local) for u, v in zip(x_peers, y_peers)]
    b_peers = [(d * u[0] + c * v[0], local) for u, v in zip(x_peers, y_peers)]
    apos, bpos = d * y + c * x, d * x + c * y

    barrier = pltpu.get_barrier_semaphore()
    everyone = [sib] + z_peers + z_cross + x_peers + y_peers
    for peer in everyone:
        pl.semaphore_signal(barrier, inc=1, device_id=peer, device_id_type=MESH)

    little = [
        pltpu.make_async_copy(src, dst, wsem.at[6 + i])
        for i, (src, dst) in enumerate(
            ((hid_hbm, hid), (ids_hbm, ids), (aff_hbm, aff), (gain_hbm, gain))
        )
    ]
    for load in little:
        load.start()
    for load in little:
        load.wait()

    values = hid[...].astype(F32)
    scale = lax.rsqrt(jnp.mean(values * values, axis=-1, keepdims=True) + 1e-06)
    s_hi = scale.astype(BF16).astype(F32)
    s_mid = (scale - s_hi).astype(BF16).astype(F32)
    s_lo = scale - s_hi - s_mid
    weight = aff[...].astype(F32)
    mix = 2.5 * weight / jnp.sum(weight, axis=-1, keepdims=True)
    m_hi = mix.astype(BF16).astype(F32)
    m_lo = mix - m_hi
    named = ids[...].astype(F32)
    rows = hid.shape[0]
    lane = lax.broadcasted_iota(jnp.int32, (rows, META), 1)
    place = (z * 2 * rows + c * rows + lax.broadcasted_iota(jnp.int32, (rows, META), 0)).astype(F32)
    meta = jnp.where(lane == 16, place, 0.0)
    meta = jnp.where(lane == 17, 1.0, meta)
    meta = jnp.where(lane == 18, s_hi, meta)
    meta = jnp.where(lane == 19, s_mid, meta)
    meta = jnp.where(lane == 20, s_lo, meta)
    for k in range(TOP):
        meta = jnp.where(lane == k, named[:, k : k + 1], meta)
        meta = jnp.where(lane == 8 + k, m_hi[:, k : k + 1], meta)
        meta = jnp.where(lane == 24 + k, m_lo[:, k : k + 1], meta)
    quarter = half // 2
    eighth = quarter // 2

    def laid(h, start):
        cols = lambda i: pl.ds(pl.multiple_of(h * half + start + i * eighth, 128), eighth)
        return jnp.concatenate([hid[:, cols(i)].astype(F32) for i in range(2)], axis=0)

    beside = jnp.concatenate([meta, jnp.zeros((rows, META), F32)], axis=0).astype(BF16)
    za[c, local, :, :eighth] = laid(c, quarter).astype(BF16)
    za[c, local, :, eighth:] = beside
    zb[c, local] = laid(c, 0).astype(BF16)
    pa[:, :eighth] = laid(d, quarter).astype(BF16)
    pa[:, eighth:] = beside
    pb[...] = laid(d, 0).astype(BF16)
    pl.semaphore_wait(barrier, len(everyone))
    def hand_out(part):
        mine, other, held = ((za.at[c, local], pa, za), (zb.at[c, local], pb, zb))[part]
        batch = []
        for index, device in enumerate(z_peers + z_cross + [sib]):
            whose = c if index < 3 else d
            sem = part * 7 + index
            copy = remote(
                mine if index < 3 else other,
                held.at[whose, local],
                zsend.at[sem],
                zrecv.at[sem],
                device,
            )
            copy.start()
            batch.append(copy)
        return batch

    def sent(batch):
        for copy in batch:
            copy.wait_send()

    loads = [
        pltpu.make_async_copy(src, dst, wsem.at[i])
        for i, (src, dst) in enumerate(
            (
                (sgate_hbm, sg),
                (sup_hbm, su),
                (gate_hbm.at[0], wg),
                (up_hbm.at[0], wu),
                (sdown_hbm, sd),
                (down_hbm, wd),
            )
        )
    ]
    batch = hand_out(0)
    sent(batch)
    first = hand_out(1)
    for load in loads:
        load.start()

    def gathered(part):
        held = (za, zb)[part]
        back = (3, 1, 2)
        origins = [step(z, by) * 2 + c for by in back] + [step(z, by) * 2 + d for by in back]
        origins.append(z * 2 + d)
        for index, origin in enumerate(origins):
            sem = part * 7 + index
            ref = held.at[c, origin]
            remote(ref, ref, zsend.at[sem], zrecv.at[sem], sib).wait_recv()
        copy = remote(held.at[c], held.at[c], zsend.at[14 + part], zrecv.at[14 + part], sib)
        first.append(copy)
        return copy

    block = RING * 2 * rows
    ahead = pl.ds(quarter, quarter + META)
    behind = pl.ds(0, quarter)

    def spread_out(held):
        v = held.astype(F32).reshape(2 * RING, 2, rows, held.shape[2])
        return [v[:, i].reshape(block, held.shape[2]) for i in range(2)]

    def normed(h, part):
        lead, rest = spread_out((za, zb)[part][h])
        info = spread_out(za[h, :, :, eighth:])[0]
        by = info[:, 18:19] + info[:, 19:20] + info[:, 20:21]
        start = (quarter, 0)[part]
        lead = lead[:, :eighth] * by * gain[h, :, start : start + eighth]
        rest = rest[:, :eighth] * by * gain[h, :, start + eighth : start + quarter]
        return jnp.concatenate([lead, rest], axis=1).astype(BF16)

    part_rows = block // 2
    upper, lower = pl.ds(0, part_rows), pl.ds(part_rows, part_rows)
    a_prev, a_next, a_far = step(apos, 3), step(apos, 1), step(apos, 2)

    def ring(part, place, rows_of, index, device):
        ref = xa.at[place, rows_of, (ahead, behind)[part]]
        sem = part * 6 + index
        return remote(ref, ref, asend.at[sem], arecv.at[sem], device)

    around = []

    def go(copy):
        copy.start()
        around.append(copy)

    def ring_first(part):
        batch = [
            ring(part, apos, upper, 0, a_peers[0]),
            ring(part, apos, lower, 1, a_peers[1]),
        ]
        for copy in batch:
            copy.start()
        return batch

    def ring_second(part):
        go(ring(part, apos, lower, 2, a_peers[0]))
        go(ring(part, apos, upper, 3, a_peers[1]))

    def ring_on(part):
        ring(part, a_prev, upper, 0, a_peers[0]).wait_recv()
        go(ring(part, a_prev, upper, 4, a_peers[0]))
        ring(part, a_next, lower, 1, a_peers[1]).wait_recv()
        go(ring(part, a_next, lower, 5, a_peers[1]))

    def ring_end(part):
        ring(part, a_prev, lower, 2, a_peers[0]).wait_recv()
        ring(part, a_next, upper, 3, a_peers[1]).wait_recv()
        ring(part, a_far, upper, 4, a_peers[0]).wait_recv()
        ring(part, a_far, lower, 5, a_peers[1]).wait_recv()

    share = gathered(0)
    xa[apos, :, quarter:half] = normed(c, 0)
    xa[apos, :, half:] = spread_out(za[c, :, :, eighth:])[0].astype(BF16)
    batch = ring_first(0)
    share.start()
    sent(batch)
    ring_second(0)
    share = gathered(1)
    xa[apos, :, :quarter] = normed(c, 1)
    batch = ring_first(1)
    share.start()
    ring_on(0)
    sent(batch)
    ring_second(1)
    ring_on(1)
    ring_end(0)

    tokens = RING * block
    info = xa[:, :, half:].reshape(tokens, META).astype(F32)
    lane = lax.broadcasted_iota(jnp.int32, (tokens, META), 1).astype(F32)
    names = jnp.zeros((tokens, META), F32)
    for k in range(TOP):
        names = jnp.where(info[:, k : k + 1] == lane, 1.0, names)
    t_row = lax.broadcasted_iota(jnp.int32, (tokens, tokens), 0)
    t_col = lax.broadcasted_iota(jnp.int32, (tokens, tokens), 1)
    earlier = jnp.where((t_col < t_row) & (t_col // block == t_row // block), 1.0, 0.0)
    counts = dot(earlier.astype(BF16), names.astype(BF16))
    base = (lax.broadcasted_iota(jnp.int32, (tokens, META), 0) // (2 * block) * CAP).astype(F32)
    ct[...] = jnp.where(names > 0.5, counts + base, -1.0).T

    duo = 2 * CAP
    tile = 256
    slot_no = lax.broadcasted_iota(jnp.int32, (duo, tokens), 0).astype(F32)
    parity = lax.rem(lax.broadcasted_iota(jnp.int32, (duo, tokens), 1) // block, 2)
    routed = []

    def choose(group):
        for by in range(RING):
            there = step(bpos, by)
            expert = (d * (y * RING + there) + c * (there * RING + x)) * 2 + z // 2
            hit = (ct[pl.ds(expert, 1), :] == slot_no) & (parity == lax.rem(bpos + group, 2))
            pm[group, by * duo : (by + 1) * duo] = jnp.where(hit, 1.0, 0.0).astype(BF16)

    def pick(group, part):
        def put(cols, width):
            seen = xa[:, :, cols].reshape(tokens, width)
            picked = dot(pm[group], seen).astype(BF16)
            rh[c, group, bpos, :, cols] = picked[:duo]
            for i in range(3):
                cs[group, i, :, cols] = picked[(i + 1) * duo : (i + 2) * duo]

        start = (quarter, 0)[part]

        put(pl.ds(start, quarter), quarter)
        if part == 0:
            put(pl.ds(half, META), META)
    def send_all(group, part):
        batch = [send(group, index, part) for index in (2, 0, 1)]
        for copy in batch:
            copy.start()
        return batch

    def send(group, index, part):
        sem = (group * 2 + part) * 3 + index
        cols = (ahead, behind)[part]
        copy = remote(
            cs.at[group, moves[index] - 1, :, cols],
            rh.at[c, group, bpos, :, cols],
            csend.at[sem],
            crecv.at[sem],
            b_peers[index],
        )
        return copy

    def kept(h, group, place, part, index):
        sem = 12 + (group * 2 + part) * 4 + index
        ref = rh.at[h, group, place, :, (ahead, behind)[part]]
        return remote(ref, ref, csend.at[sem], crecv.at[sem], sib)

    def give(group, place, part, index):
        copy = kept(c, group, place, part, index)
        copy.start()
        routed.append(copy)

    choose(0)
    pick(0, 0)
    batches = [send_all(0, 0)]
    give(0, bpos, 0, 0)
    choose(1)
    ring_end(1)
    pick(0, 1)
    batches.append(send_all(0, 1))
    give(0, bpos, 1, 0)
    pick(1, 0)
    pick(1, 1)
    for part, held in enumerate((za, zb)):
        ref = held.at[d]
        remote(ref, ref, zsend.at[14 + part], zrecv.at[14 + part], sib).wait_recv()
    xo[:, quarter:] = normed(d, 0)
    xo[:, :quarter] = normed(d, 1)

    loads[0].wait()
    loads[1].wait()
    own_rows = pl.ds(pl.multiple_of(c * half, 128), half)
    other_rows = pl.ds(pl.multiple_of(d * half, 128), half)
    mine = xa[apos, :, :half]
    s_gate = dot(mine, sg[own_rows, :]) + dot(xo[...], sg[other_rows, :])
    s_up = dot(mine, su[own_rows, :]) + dot(xo[...], su[other_rows, :])
    sa[c, z] = (s_gate / (1.0 + jnp.exp(-s_gate)) * s_up).astype(BF16)
    sh = Gather(lambda q: sa.at[c, q], z, z_peers, ssend, srecv, sib)
    sh.start()
    for part in range(2):
        sent(batches[part])
        routed += send_all(1, part)
        give(1, bpos, part, 0)
    oo[:, :, 2 * duo : META] = jnp.zeros((2, 2, META - 2 * duo, oo.shape[3]), BF16)
    oo[:, :, META + 2 * duo :] = jnp.zeros((2, 2, META - 2 * duo, oo.shape[3]), BF16)

    def collect(group):
        for part in range(2):
            for index, by in ((0, 3), (1, 1), (2, 2)):
                place = step(bpos, by)
                sem = (group * 2 + part) * 3 + index
                ref = rh.at[c, group, place, :, (ahead, behind)[part]]
                remote(ref, ref, csend.at[sem], crecv.at[sem], sib).wait_recv()
                give(group, place, part, index + 1)
        for part in range(2):
            for index, by in ((0, 0), (1, 3), (2, 1), (3, 2)):
                kept(d, group, step(apos, by), part, index).wait_recv()

    slots = RING * duo
    expert = (node * 2 + z // 2).astype(F32)

    def turned(v, group):
        pieces = []
        for xx in range(RING):
            for k in range(2):
                at = (2 * k + (xx + group) % 2) * 2 + xx // 2
                pieces.append(v[at * CAP : (at + 1) * CAP])
        return jnp.concatenate(pieces, axis=0)

    def hidden(group):
        info = rh[0, group, :, :, half:].reshape(slots, META).astype(F32)
        lane = lax.broadcasted_iota(jnp.int32, (slots, META), 1)
        shares = pltpu.roll(info, META - 8, 1) + pltpu.roll(info, META - 24, 1)
        factor = jnp.sum(
            jnp.where((lane < TOP) & (info == expert), shares, 0.0), axis=1, keepdims=True
        )
        s_no = lax.broadcasted_iota(jnp.int32, (slots, 1), 0)
        home = (lax.rem(s_no // CAP, RING) * block).astype(F32)
        token = jnp.where(info[:, 17:18] > 0.5, info[:, 16:17] + home, -1.0)
        for i in range(2):
            column = jnp.broadcast_to(token[i * 2 * duo : (i + 1) * 2 * duo], (2 * duo, META))
            column = jnp.concatenate(
                [column, jnp.full((META - 2 * duo, META), -1.0, F32)], axis=0
            )
            ac[c, z, group, slots:, i * META : (i + 1) * META] = column.T[:16].astype(BF16)
        ac[c, z, group, slots:, 2 * META :] = jnp.zeros((16, ac.shape[4] - 2 * META), BF16)

        gathers = []
        for j in range(wg.shape[1] // tile):
            cols = pl.ds(j * tile, tile)
            one = rh[0, group, :, :, :half].reshape(slots, half)
            two = rh[1, group, :, :, :half].reshape(slots, half)
            g = dot(one, wg[:half, cols]) + turned(dot(two, wg[half:, cols]), group)
            u = dot(one, wu[:half, cols]) + turned(dot(two, wu[half:, cols]), group)
            ac[c, z, group, :slots, cols] = (g / (1.0 + jnp.exp(-g)) * u * factor).astype(BF16)
            gather = Gather(
                lambda q, cols=cols: ac.at[c, q, group, :, cols],
                z,
                z_peers,
                gsend.at[group, j],
                grecv.at[group, j],
                sib,
            )
            if group == 1:
                gg[0][j].settle()
            gather.start()
            gathers.append(gather)
        return gathers

    collect(0)
    loads[2].wait()
    loads[3].wait()
    gg = [hidden(0)]
    collect(1)
    gg.append(hidden(1))
    width = oo.shape[3]
    deep = ac.shape[4]
    ht = block // 2
    row_no = lax.broadcasted_iota(jnp.int32, (tokens, META), 0).astype(F32)

    def outputs(group, j):
        gg[group][j].arrive()
        gg[group][j].shared(lambda q: ac.at[d, q, group, :, pl.ds(j * tile, tile)])
        for e in range(2):
            for lo in range(0, width, tile):
                hi = min(lo + tile, width)
                res = jnp.zeros((slots, hi - lo), F32) if j == 0 else acc[e, :, lo:hi]
                for zz in range(2):
                    for cc in range(2):
                        at = (zz * 2 + cc) * deep + j * tile
                        res += dot(
                            ac[cc, e * 2 + zz, group, :slots, j * tile : (j + 1) * tile],
                            wd[e, at : at + tile, lo:hi],
                        )
                if j == 0:
                    acc[e, :, lo:hi] = res
                    continue
                for i in range(2):
                    oo[group, i, e * META : e * META + 2 * duo, lo:hi] = res[
                        i * 2 * duo : (i + 1) * 2 * duo
                    ].astype(BF16)

    def combine(group):
        for i in range(2):
            spread = [
                jnp.where(
                    ac[0, e * 2, group, slots : slots + 1, i * META : (i + 1) * META].astype(F32)
                    == row_no,
                    1.0,
                    0.0,
                ).astype(BF16)
                for e in range(2)
            ]
            sums = dot(jnp.concatenate(spread, axis=1), oo[group, i]).astype(BF16)
            for p in range(2):
                for k in range(2):
                    xx = i * 2 + p
                    yy = 2 * k + (xx + group) % 2
                    at = (p * 2 + k) * block
                    pp[0, group, xx, k] = sums[at : at + ht]
                    pp[1, group, yy, i] = sums[at + ht : at + block]

    axes = ((x, x_peers), (y, y_peers))
    sums1, sums2 = [], []

    def spread_first(group):
        for h in range(2):
            pos, peers = axes[h]
            for index, by in enumerate(moves):
                sem = (group * 2 + h) * 3 + index
                copy = remote(
                    pp.at[h, group, step(pos, by)],
                    r1.at[h, group, index],
                    rsend.at[sem],
                    rrecv.at[sem],
                    peers[index],
                )
                copy.start()
                sums1.append(copy)

    def sum_first(group):
        for h in range(2):
            pos = axes[h][0]
            for index in range(3):
                sums1[(group * 2 + h) * 3 + index].wait_recv()
            whole = pp[h, group, pos].astype(F32)
            for index in range(3):
                whole += r1[h, group, index].astype(F32)
            for k in range(2):
                t1[h, 2 * k + lax.rem(pos + group, 2)] = whole[k].astype(BF16)

    loads[5].wait()
    outputs(0, 0)
    outputs(0, 1)
    combine(0)
    spread_first(0)
    sh.arrive()
    sh.shared(lambda q: sa.at[d, q])
    loads[4].wait()
    total = jnp.zeros(sres.shape, F32)
    wide = sa.shape[3]
    for zz in range(RING):
        for cc in range(2):
            total += dot(sa[cc, zz], sd[(zz * 2 + cc) * wide : (zz * 2 + cc + 1) * wide, :])
    sres[...] = total

    outputs(1, 0)
    outputs(1, 1)
    combine(1)
    spread_first(1)
    sum_first(0)
    sum_first(1)
    for h in range(2):
        pos, peers = axes[1 - h]
        for index, by in enumerate(moves):
            sem = 12 + h * 3 + index
            copy = remote(
                t1.at[h, step(pos, by)],
                r2.at[h, index],
                rsend.at[sem],
                rrecv.at[sem],
                peers[index],
            )
            copy.start()
            sums2.append(copy)
    fore = spread_out(za[z // 2, :, :, :eighth])
    aft = spread_out(zb[z // 2])
    late = lax.rem(z, 2) == 1
    left = jnp.where(
        late,
        jnp.where(c == 0, fore[0], fore[1]),
        jnp.where(c == 0, aft[0], aft[1]),
    )
    left = left + sres[...]
    for h in range(2):
        pos = axes[1 - h][0]
        whole = left[h * ht : (h + 1) * ht] + t1[h, pos].astype(F32)
        for index in range(3):
            sums2[h * 3 + index].wait_recv()
            whole += r2[h, index].astype(F32)
        out[h * ht : (h + 1) * ht] = whole.astype(BF16)

    for gather in [sh] + gg[0] + gg[1]:
        gather.drain()
    for copy in first + around + routed + sums1 + sums2:
        copy.wait_send()


def body(hid, ids, aff, gain, gate, up, down, sgate, sup, sdown):
    rows, width = hid.shape
    half = width // 2
    block = rows * 2 * RING
    units = gate.shape[2]
    cols = down.shape[2]
    shared = sgate.shape[1]
    duo = 2 * CAP
    slots = RING * duo
    ht = block // 2
    dma = pltpu.SemaphoreType.DMA
    hbm = pl.BlockSpec(memory_space=pl.ANY)
    vmem = pl.BlockSpec(memory_space=pltpu.VMEM)
    return pl.pallas_call(
        kernel,
        out_shape=jax.ShapeDtypeStruct((block, cols), BF16),
        in_specs=[hbm] * 10,
        out_specs=vmem,
        scratch_shapes=[
            pltpu.VMEM(hid.shape, BF16),
            pltpu.VMEM(ids.shape, jnp.int32),
            pltpu.VMEM(aff.shape, BF16),
            pltpu.VMEM((2, 1, half), F32),
            pltpu.VMEM((width, units), BF16),
            pltpu.VMEM((width, units), BF16),
            pltpu.VMEM(down.shape, BF16),
            pltpu.VMEM(sgate.shape, BF16),
            pltpu.VMEM(sup.shape, BF16),
            pltpu.VMEM(sdown.shape, BF16),
            pltpu.VMEM((2 * rows, half // 4 + META), BF16),
            pltpu.VMEM((2 * rows, half // 4), BF16),
            pltpu.VMEM((2, 2 * RING, 2 * rows, half // 4 + META), BF16),
            pltpu.VMEM((2, 2 * RING, 2 * rows, half // 4), BF16),
            pltpu.VMEM((RING, block, half + META), BF16),
            pltpu.VMEM((block, half), BF16),
            pltpu.VMEM((META, RING * block), F32),
            pltpu.VMEM((2, slots, RING * block), BF16),
            pltpu.VMEM((2, 3, duo, half + META), BF16),
            pltpu.VMEM((2, 2, RING, duo, half + META), BF16),
            pltpu.VMEM((2, RING, 2, slots + 16, units), BF16),
            pltpu.VMEM((2, RING, block, shared), BF16),
            pltpu.VMEM((block, cols), F32),
            pltpu.VMEM((2, slots, cols), F32),
            pltpu.VMEM((2, 2, 2 * META, cols), BF16),
            pltpu.VMEM((2, 2, RING, 2, ht, cols), BF16),
            pltpu.VMEM((2, 2, 3, 2, ht, cols), BF16),
            pltpu.VMEM((2, 3, ht, cols), BF16),
            pltpu.VMEM((2, RING, ht, cols), BF16),
            dma((10,)),
            dma((16,)),
            dma((16,)),
            dma((12,)),
            dma((12,)),
            dma((7,)),
            dma((7,)),
            dma((28,)),
            dma((28,)),
            dma((2, 2, 7)),
            dma((2, 2, 7)),
            dma((18,)),
            dma((18,)),
        ],
        compiler_params=pltpu.CompilerParams(
            collective_id=0, has_side_effects=True, vmem_limit_bytes=63 * 1024 * 1024
        ),
    )(hid, ids, aff, gain.reshape(2, 1, half), gate, up, down, sgate, sup, sdown)


def solution(mesh):
    in_specs = (
        P(("node", "local"), None),
        P(("node", "local"), None),
        P(("node", "local"), None),
        P(),
        P(("node", "local"), None, None),
        P(("node", "local"), None, None),
        P("node", None, "local"),
        P(None, "local"),
        P(None, "local"),
        P(None, "local"),
    )
    return jax.shard_map(
        body, mesh=mesh, in_specs=in_specs, out_specs=P("node", "local"), check_vma=False
    )
```

```python
import functools

import jax
import jax.numpy as jnp
from jax import lax
from jax.experimental import pallas as pl
from jax.experimental.pallas import tpu as pltpu
from jax.sharding import PartitionSpec as P

MESH = pl.DeviceIdType.MESH
F32 = jnp.float32
BF16 = jnp.bfloat16
RING = 4
META = 128
CAP = 24
TOP = 8


def remote(src, dst, send, recv, device):
    return pltpu.make_async_remote_copy(
        src_ref=src,
        dst_ref=dst,
        send_sem=send,
        recv_sem=recv,
        device_id=device,
        device_id_type=MESH,
    )


def dot(a, b):
    return jnp.dot(a, b, preferred_element_type=F32)


class Gather:
    def __init__(self, slot, pos, peers, send, recv, other):
        self.slot, self.pos, self.peers, self.other = slot, pos, peers, other
        self.send, self.recv = send, recv
        self.origins = [lax.rem(pos + step, RING) for step in (3, 1, 2)]
        self.sent = []

    def copy(self, ref, index, device):
        return remote(ref, ref, self.send.at[index], self.recv.at[index], device)

    def go(self, ref, index, device):
        copy = self.copy(ref, index, device)
        copy.start()
        self.sent.append(copy)

    def start(self):
        for index, device in enumerate(self.peers):
            self.go(self.slot(self.pos), index, device)
        self.go(self.slot(self.pos), 3, self.other)

    def arrive(self):
        for index, origin in enumerate(self.origins):
            self.copy(self.slot(origin), index, self.other).wait_recv()
            self.go(self.slot(origin), 4 + index, self.other)

    def shared(self, mirror):
        for index, origin in enumerate([self.pos] + self.origins):
            self.copy(mirror(origin), 3 + index, self.other).wait_recv()

    def drain(self):
        for copy in self.sent:
            copy.wait_send()


def kernel(
    hid_hbm,
    ids_hbm,
    aff_hbm,
    gain_hbm,
    gate_hbm,
    up_hbm,
    down_hbm,
    sgate_hbm,
    sup_hbm,
    sdown_hbm,
    out,
    hid,
    ids,
    aff,
    gain,
    wg,
    wu,
    wd,
    sg,
    su,
    sd,
    pa,
    pb,
    za,
    zb,
    xa,
    xo,
    ct,
    pm,
    cs,
    rh,
    ac,
    sa,
    sres,
    acc,
    oo,
    pp,
    r1,
    r2,
    t1,
    wsem,
    zsend,
    zrecv,
    asend,
    arecv,
    ssend,
    srecv,
    csend,
    crecv,
    gsend,
    grecv,
    rsend,
    rrecv,
):
    half = hid.shape[1] // 2
    node, local = lax.axis_index("node"), lax.axis_index("local")
    y, x = node // RING, lax.rem(node, RING)
    z, c = local // 2, lax.rem(local, 2)
    d = 1 - c
    sib = (node, z * 2 + d)
    moves = (1, 3, 2)
    step = lambda v, by: lax.rem(v + by, RING)
    z_peers = [(node, step(z, by) * 2 + c) for by in moves]
    x_peers = [(y * RING + step(x, by), local) for by in moves]
    y_peers = [(step(y, by) * RING + x, local) for by in moves]
    z_cross = [(node, step(z, by) * 2 + d) for by in moves]
    a_peers = [(d * v[0] + c * u[0], local) for u, v in zip(x_peers, y_peers)]
    b_peers = [(d * u[0] + c * v[0], local) for u, v in zip(x_peers, y_peers)]
    apos, bpos = d * y + c * x, d * x + c * y

    barrier = pltpu.get_barrier_semaphore()
    everyone = [sib] + z_peers + z_cross + x_peers + y_peers
    for peer in everyone:
        pl.semaphore_signal(barrier, inc=1, device_id=peer, device_id_type=MESH)

    little = [
        pltpu.make_async_copy(src, dst, wsem.at[6 + i])
        for i, (src, dst) in enumerate(
            ((hid_hbm, hid), (ids_hbm, ids), (aff_hbm, aff), (gain_hbm, gain))
        )
    ]
    for load in little:
        load.start()
    for load in little:
        load.wait()

    values = hid[...].astype(F32)
    scale = lax.rsqrt(jnp.mean(values * values, axis=-1, keepdims=True) + 1e-06)
    s_hi = scale.astype(BF16).astype(F32)
    s_mid = (scale - s_hi).astype(BF16).astype(F32)
    s_lo = scale - s_hi - s_mid
    weight = aff[...].astype(F32)
    mix = 2.5 * weight / jnp.sum(weight, axis=-1, keepdims=True)
    m_hi = mix.astype(BF16).astype(F32)
    m_lo = mix - m_hi
    named = ids[...].astype(F32)
    rows = hid.shape[0]
    lane = lax.broadcasted_iota(jnp.int32, (rows, META), 1)
    place = (z * 2 * rows + c * rows + lax.broadcasted_iota(jnp.int32, (rows, META), 0)).astype(F32)
    meta = jnp.where(lane == 16, place, 0.0)
    meta = jnp.where(lane == 17, 1.0, meta)
    meta = jnp.where(lane == 18, s_hi, meta)
    meta = jnp.where(lane == 19, s_mid, meta)
    meta = jnp.where(lane == 20, s_lo, meta)
    for k in range(TOP):
        meta = jnp.where(lane == k, named[:, k : k + 1], meta)
        meta = jnp.where(lane == 8 + k, m_hi[:, k : k + 1], meta)
        meta = jnp.where(lane == 24 + k, m_lo[:, k : k + 1], meta)
    quarter = half // 2
    eighth = quarter // 2

    def laid(h, start):
        cols = lambda i: pl.ds(pl.multiple_of(h * half + start + i * eighth, 128), eighth)
        return jnp.concatenate([hid[:, cols(i)].astype(F32) for i in range(2)], axis=0)

    beside = jnp.concatenate([meta, jnp.zeros((rows, META), F32)], axis=0).astype(BF16)
    za[c, local, :, :eighth] = laid(c, quarter).astype(BF16)
    za[c, local, :, eighth:] = beside
    zb[c, local] = laid(c, 0).astype(BF16)
    pa[:, :eighth] = laid(d, quarter).astype(BF16)
    pa[:, eighth:] = beside
    pb[...] = laid(d, 0).astype(BF16)
    pl.semaphore_wait(barrier, len(everyone))
    def hand_out(part):
        mine, other, held = ((za.at[c, local], pa, za), (zb.at[c, local], pb, zb))[part]
        batch = []
        for index, device in enumerate(z_peers + z_cross + [sib]):
            whose = c if index < 3 else d
            sem = part * 7 + index
            copy = remote(
                mine if index < 3 else other,
                held.at[whose, local],
                zsend.at[sem],
                zrecv.at[sem],
                device,
            )
            copy.start()
            batch.append(copy)
        return batch

    def sent(batch):
        for copy in batch:
            copy.wait_send()

    loads = [
        pltpu.make_async_copy(src, dst, wsem.at[i])
        for i, (src, dst) in enumerate(
            (
                (sgate_hbm, sg),
                (sup_hbm, su),
                (gate_hbm.at[0], wg),
                (up_hbm.at[0], wu),
                (sdown_hbm, sd),
                (down_hbm, wd),
            )
        )
    ]
    batch = hand_out(0)
    sent(batch)
    first = hand_out(1)
    for load in loads:
        load.start()

    def gathered(part):
        held = (za, zb)[part]
        back = (3, 1, 2)
        origins = [step(z, by) * 2 + c for by in back] + [step(z, by) * 2 + d for by in back]
        origins.append(z * 2 + d)
        for index, origin in enumerate(origins):
            sem = part * 7 + index
            ref = held.at[c, origin]
            remote(ref, ref, zsend.at[sem], zrecv.at[sem], sib).wait_recv()
        copy = remote(held.at[c], held.at[c], zsend.at[14 + part], zrecv.at[14 + part], sib)
        first.append(copy)
        return copy

    block = RING * 2 * rows
    ahead = pl.ds(quarter, quarter + META)
    behind = pl.ds(0, quarter)

    def spread_out(held):
        v = held.astype(F32).reshape(2 * RING, 2, rows, held.shape[2])
        return [v[:, i].reshape(block, held.shape[2]) for i in range(2)]

    def normed(h, part):
        lead, rest = spread_out((za, zb)[part][h])
        info = spread_out(za[h, :, :, eighth:])[0]
        by = info[:, 18:19] + info[:, 19:20] + info[:, 20:21]
        start = (quarter, 0)[part]
        lead = lead[:, :eighth] * by * gain[h, :, start : start + eighth]
        rest = rest[:, :eighth] * by * gain[h, :, start + eighth : start + quarter]
        return jnp.concatenate([lead, rest], axis=1).astype(BF16)

    part_rows = block // 2
    upper, lower = pl.ds(0, part_rows), pl.ds(part_rows, part_rows)
    a_prev, a_next, a_far = step(apos, 3), step(apos, 1), step(apos, 2)

    def ring(part, place, rows_of, index, device):
        ref = xa.at[place, rows_of, (ahead, behind)[part]]
        sem = part * 6 + index
        return remote(ref, ref, asend.at[sem], arecv.at[sem], device)

    around = []

    def go(copy):
        copy.start()
        around.append(copy)

    def ring_first(part):
        batch = [
            ring(part, apos, upper, 0, a_peers[0]),
            ring(part, apos, lower, 1, a_peers[1]),
        ]
        for copy in batch:
            copy.start()
        return batch

    def ring_second(part):
        go(ring(part, apos, lower, 2, a_peers[0]))
        go(ring(part, apos, upper, 3, a_peers[1]))

    def ring_on(part):
        ring(part, a_prev, upper, 0, a_peers[0]).wait_recv()
        go(ring(part, a_prev, upper, 4, a_peers[0]))
        ring(part, a_next, lower, 1, a_peers[1]).wait_recv()
        go(ring(part, a_next, lower, 5, a_peers[1]))

    def ring_end(part):
        ring(part, a_prev, lower, 2, a_peers[0]).wait_recv()
        ring(part, a_next, upper, 3, a_peers[1]).wait_recv()
        ring(part, a_far, upper, 4, a_peers[0]).wait_recv()
        ring(part, a_far, lower, 5, a_peers[1]).wait_recv()

    share = gathered(0)
    xa[apos, :, quarter:half] = normed(c, 0)
    xa[apos, :, half:] = spread_out(za[c, :, :, eighth:])[0].astype(BF16)
    batch = ring_first(0)
    share.start()
    sent(batch)
    ring_second(0)
    share = gathered(1)
    xa[apos, :, :quarter] = normed(c, 1)
    batch = ring_first(1)
    share.start()
    ring_on(0)
    sent(batch)
    ring_second(1)
    ring_on(1)
    ring_end(0)

    tokens = RING * block
    info = xa[:, :, half:].reshape(tokens, META).astype(F32)
    lane = lax.broadcasted_iota(jnp.int32, (tokens, META), 1).astype(F32)
    names = jnp.zeros((tokens, META), F32)
    for k in range(TOP):
        names = jnp.where(info[:, k : k + 1] == lane, 1.0, names)
    t_row = lax.broadcasted_iota(jnp.int32, (tokens, tokens), 0)
    t_col = lax.broadcasted_iota(jnp.int32, (tokens, tokens), 1)
    earlier = jnp.where((t_col < t_row) & (t_col // block == t_row // block), 1.0, 0.0)
    counts = dot(earlier.astype(BF16), names.astype(BF16))
    base = (lax.broadcasted_iota(jnp.int32, (tokens, META), 0) // (2 * block) * CAP).astype(F32)
    ct[...] = jnp.where(names > 0.5, counts + base, -1.0).T

    duo = 2 * CAP
    tile = 256
    slot_no = lax.broadcasted_iota(jnp.int32, (duo, tokens), 0).astype(F32)
    parity = lax.rem(lax.broadcasted_iota(jnp.int32, (duo, tokens), 1) // block, 2)
    routed = []

    def choose(group):
        for by in range(RING):
            there = step(bpos, by)
            expert = (d * (y * RING + there) + c * (there * RING + x)) * 2 + z // 2
            hit = (ct[pl.ds(expert, 1), :] == slot_no) & (parity == lax.rem(bpos + group, 2))
            pm[group, by * duo : (by + 1) * duo] = jnp.where(hit, 1.0, 0.0).astype(BF16)

    def pick(group, part):
        def put(cols, width):
            seen = xa[:, :, cols].reshape(tokens, width)
            picked = dot(pm[group], seen).astype(BF16)
            rh[c, group, bpos, :, cols] = picked[:duo]
            for i in range(3):
                cs[group, i, :, cols] = picked[(i + 1) * duo : (i + 2) * duo]

        start = (quarter, 0)[part]

        put(pl.ds(start, quarter), quarter)
        if part == 0:
            put(pl.ds(half, META), META)
    def send_all(group, part):
        batch = [send(group, index, part) for index in (2, 0, 1)]
        for copy in batch:
            copy.start()
        return batch

    def send(group, index, part):
        sem = (group * 2 + part) * 3 + index
        cols = (ahead, behind)[part]
        copy = remote(
            cs.at[group, moves[index] - 1, :, cols],
            rh.at[c, group, bpos, :, cols],
            csend.at[sem],
            crecv.at[sem],
            b_peers[index],
        )
        return copy

    def kept(h, group, place, part, index):
        sem = 12 + (group * 2 + part) * 4 + index
        ref = rh.at[h, group, place, :, (ahead, behind)[part]]
        return remote(ref, ref, csend.at[sem], crecv.at[sem], sib)

    def give(group, place, part, index):
        copy = kept(c, group, place, part, index)
        copy.start()
        routed.append(copy)

    choose(0)
    pick(0, 0)
    batches = [send_all(0, 0)]
    give(0, bpos, 0, 0)
    choose(1)
    ring_end(1)
    pick(0, 1)
    batches.append(send_all(0, 1))
    give(0, bpos, 1, 0)
    pick(1, 0)
    pick(1, 1)
    for part, held in enumerate((za, zb)):
        ref = held.at[d]
        remote(ref, ref, zsend.at[14 + part], zrecv.at[14 + part], sib).wait_recv()
    xo[:, quarter:] = normed(d, 0)
    xo[:, :quarter] = normed(d, 1)

    loads[0].wait()
    loads[1].wait()
    own_rows = pl.ds(pl.multiple_of(c * half, 128), half)
    other_rows = pl.ds(pl.multiple_of(d * half, 128), half)
    mine = xa[apos, :, :half]
    s_gate = dot(mine, sg[own_rows, :]) + dot(xo[...], sg[other_rows, :])
    s_up = dot(mine, su[own_rows, :]) + dot(xo[...], su[other_rows, :])
    sa[c, z] = (s_gate / (1.0 + jnp.exp(-s_gate)) * s_up).astype(BF16)
    sh = Gather(lambda q: sa.at[c, q], z, z_peers, ssend, srecv, sib)
    sh.start()
    for part in range(2):
        sent(batches[part])
        routed += send_all(1, part)
        give(1, bpos, part, 0)
    oo[:, :, 2 * duo : META] = jnp.zeros((2, 2, META - 2 * duo, oo.shape[3]), BF16)
    oo[:, :, META + 2 * duo :] = jnp.zeros((2, 2, META - 2 * duo, oo.shape[3]), BF16)

    def collect(group):
        for part in range(2):
            for index, by in ((0, 3), (1, 1), (2, 2)):
                place = step(bpos, by)
                sem = (group * 2 + part) * 3 + index
                ref = rh.at[c, group, place, :, (ahead, behind)[part]]
                remote(ref, ref, csend.at[sem], crecv.at[sem], sib).wait_recv()
                give(group, place, part, index + 1)
        for part in range(2):
            for index, by in ((0, 0), (1, 3), (2, 1), (3, 2)):
                kept(d, group, step(apos, by), part, index).wait_recv()

    slots = RING * duo
    expert = (node * 2 + z // 2).astype(F32)

    def turned(v, group):
        pieces = []
        for xx in range(RING):
            for k in range(2):
                at = (2 * k + (xx + group) % 2) * 2 + xx // 2
                pieces.append(v[at * CAP : (at + 1) * CAP])
        return jnp.concatenate(pieces, axis=0)

    def hidden(group):
        info = rh[0, group, :, :, half:].reshape(slots, META).astype(F32)
        lane = lax.broadcasted_iota(jnp.int32, (slots, META), 1)
        shares = pltpu.roll(info, META - 8, 1) + pltpu.roll(info, META - 24, 1)
        factor = jnp.sum(
            jnp.where((lane < TOP) & (info == expert), shares, 0.0), axis=1, keepdims=True
        )
        s_no = lax.broadcasted_iota(jnp.int32, (slots, 1), 0)
        home = (lax.rem(s_no // CAP, RING) * block).astype(F32)
        token = jnp.where(info[:, 17:18] > 0.5, info[:, 16:17] + home, -1.0)
        for i in range(2):
            column = jnp.broadcast_to(token[i * 2 * duo : (i + 1) * 2 * duo], (2 * duo, META))
            column = jnp.concatenate(
                [column, jnp.full((META - 2 * duo, META), -1.0, F32)], axis=0
            )
            ac[c, z, group, slots:, i * META : (i + 1) * META] = column.T[:16].astype(BF16)
        ac[c, z, group, slots:, 2 * META :] = jnp.zeros((16, ac.shape[4] - 2 * META), BF16)

        gathers = []
        for j in range(wg.shape[1] // tile):
            cols = pl.ds(j * tile, tile)
            one = rh[0, group, :, :, :half].reshape(slots, half)
            two = rh[1, group, :, :, :half].reshape(slots, half)
            g = dot(one, wg[:half, cols]) + turned(dot(two, wg[half:, cols]), group)
            u = dot(one, wu[:half, cols]) + turned(dot(two, wu[half:, cols]), group)
            ac[c, z, group, :slots, cols] = (g / (1.0 + jnp.exp(-g)) * u * factor).astype(BF16)
            gather = Gather(
                lambda q, cols=cols: ac.at[c, q, group, :, cols],
                z,
                z_peers,
                gsend.at[group, j],
                grecv.at[group, j],
                sib,
            )
            gather.start()
            gathers.append(gather)
        return gathers

    collect(0)
    loads[2].wait()
    loads[3].wait()
    gg = [hidden(0)]
    collect(1)
    gg.append(hidden(1))
    width = oo.shape[3]
    deep = ac.shape[4]
    ht = block // 2
    row_no = lax.broadcasted_iota(jnp.int32, (tokens, META), 0).astype(F32)

    def outputs(group, j):
        gg[group][j].arrive()
        gg[group][j].shared(lambda q: ac.at[d, q, group, :, pl.ds(j * tile, tile)])
        for e in range(2):
            for lo in range(0, width, tile):
                hi = min(lo + tile, width)
                res = jnp.zeros((slots, hi - lo), F32) if j == 0 else acc[e, :, lo:hi]
                for zz in range(2):
                    for cc in range(2):
                        at = (zz * 2 + cc) * deep + j * tile
                        res += dot(
                            ac[cc, e * 2 + zz, group, :slots, j * tile : (j + 1) * tile],
                            wd[e, at : at + tile, lo:hi],
                        )
                if j == 0:
                    acc[e, :, lo:hi] = res
                    continue
                for i in range(2):
                    oo[group, i, e * META : e * META + 2 * duo, lo:hi] = res[
                        i * 2 * duo : (i + 1) * 2 * duo
                    ].astype(BF16)

    def combine(group):
        for i in range(2):
            spread = [
                jnp.where(
                    ac[0, e * 2, group, slots : slots + 1, i * META : (i + 1) * META].astype(F32)
                    == row_no,
                    1.0,
                    0.0,
                ).astype(BF16)
                for e in range(2)
            ]
            sums = dot(jnp.concatenate(spread, axis=1), oo[group, i]).astype(BF16)
            for p in range(2):
                for k in range(2):
                    xx = i * 2 + p
                    yy = 2 * k + (xx + group) % 2
                    at = (p * 2 + k) * block
                    pp[0, group, xx, k] = sums[at : at + ht]
                    pp[1, group, yy, i] = sums[at + ht : at + block]

    axes = ((x, x_peers), (y, y_peers))
    sums1, sums2 = [], []

    def spread_first(group):
        for h in range(2):
            pos, peers = axes[h]
            for index, by in enumerate(moves):
                sem = (group * 2 + h) * 3 + index
                copy = remote(
                    pp.at[h, group, step(pos, by)],
                    r1.at[h, group, index],
                    rsend.at[sem],
                    rrecv.at[sem],
                    peers[index],
                )
                copy.start()
                sums1.append(copy)

    def sum_first(group):
        for h in range(2):
            pos = axes[h][0]
            for index in range(3):
                sums1[(group * 2 + h) * 3 + index].wait_recv()
            whole = pp[h, group, pos].astype(F32)
            for index in range(3):
                whole += r1[h, group, index].astype(F32)
            for k in range(2):
                t1[h, 2 * k + lax.rem(pos + group, 2)] = whole[k].astype(BF16)

    loads[5].wait()
    outputs(0, 0)
    outputs(0, 1)
    combine(0)
    spread_first(0)
    sh.arrive()
    sh.shared(lambda q: sa.at[d, q])
    loads[4].wait()
    total = jnp.zeros(sres.shape, F32)
    wide = sa.shape[3]
    for zz in range(RING):
        for cc in range(2):
            total += dot(sa[cc, zz], sd[(zz * 2 + cc) * wide : (zz * 2 + cc + 1) * wide, :])
    sres[...] = total

    outputs(1, 0)
    outputs(1, 1)
    combine(1)
    spread_first(1)
    sum_first(0)
    sum_first(1)
    for h in range(2):
        pos, peers = axes[1 - h]
        for index, by in enumerate(moves):
            sem = 12 + h * 3 + index
            copy = remote(
                t1.at[h, step(pos, by)],
                r2.at[h, index],
                rsend.at[sem],
                rrecv.at[sem],
                peers[index],
            )
            copy.start()
            sums2.append(copy)
    fore = spread_out(za[z // 2, :, :, :eighth])
    aft = spread_out(zb[z // 2])
    late = lax.rem(z, 2) == 1
    left = jnp.where(
        late,
        jnp.where(c == 0, fore[0], fore[1]),
        jnp.where(c == 0, aft[0], aft[1]),
    )
    left = left + sres[...]
    for h in range(2):
        pos = axes[1 - h][0]
        whole = left[h * ht : (h + 1) * ht] + t1[h, pos].astype(F32)
        for index in range(3):
            sums2[h * 3 + index].wait_recv()
            whole += r2[h, index].astype(F32)
        out[h * ht : (h + 1) * ht] = whole.astype(BF16)

    for gather in [sh] + gg[0] + gg[1]:
        gather.drain()
    for copy in first + around + routed + sums1 + sums2:
        copy.wait_send()


def body(hid, ids, aff, gain, gate, up, down, sgate, sup, sdown):
    rows, width = hid.shape
    half = width // 2
    block = rows * 2 * RING
    units = gate.shape[2]
    cols = down.shape[2]
    shared = sgate.shape[1]
    duo = 2 * CAP
    slots = RING * duo
    ht = block // 2
    dma = pltpu.SemaphoreType.DMA
    hbm = pl.BlockSpec(memory_space=pl.ANY)
    vmem = pl.BlockSpec(memory_space=pltpu.VMEM)
    return pl.pallas_call(
        kernel,
        out_shape=jax.ShapeDtypeStruct((block, cols), BF16),
        in_specs=[hbm] * 10,
        out_specs=vmem,
        scratch_shapes=[
            pltpu.VMEM(hid.shape, BF16),
            pltpu.VMEM(ids.shape, jnp.int32),
            pltpu.VMEM(aff.shape, BF16),
            pltpu.VMEM((2, 1, half), F32),
            pltpu.VMEM((width, units), BF16),
            pltpu.VMEM((width, units), BF16),
            pltpu.VMEM(down.shape, BF16),
            pltpu.VMEM(sgate.shape, BF16),
            pltpu.VMEM(sup.shape, BF16),
            pltpu.VMEM(sdown.shape, BF16),
            pltpu.VMEM((2 * rows, half // 4 + META), BF16),
            pltpu.VMEM((2 * rows, half // 4), BF16),
            pltpu.VMEM((2, 2 * RING, 2 * rows, half // 4 + META), BF16),
            pltpu.VMEM((2, 2 * RING, 2 * rows, half // 4), BF16),
            pltpu.VMEM((RING, block, half + META), BF16),
            pltpu.VMEM((block, half), BF16),
            pltpu.VMEM((META, RING * block), F32),
            pltpu.VMEM((2, slots, RING * block), BF16),
            pltpu.VMEM((2, 3, duo, half + META), BF16),
            pltpu.VMEM((2, 2, RING, duo, half + META), BF16),
            pltpu.VMEM((2, RING, 2, slots + 16, units), BF16),
            pltpu.VMEM((2, RING, block, shared), BF16),
            pltpu.VMEM((block, cols), F32),
            pltpu.VMEM((2, slots, cols), F32),
            pltpu.VMEM((2, 2, 2 * META, cols), BF16),
            pltpu.VMEM((2, 2, RING, 2, ht, cols), BF16),
            pltpu.VMEM((2, 2, 3, 2, ht, cols), BF16),
            pltpu.VMEM((2, 3, ht, cols), BF16),
            pltpu.VMEM((2, RING, ht, cols), BF16),
            dma((10,)),
            dma((16,)),
            dma((16,)),
            dma((12,)),
            dma((12,)),
            dma((7,)),
            dma((7,)),
            dma((28,)),
            dma((28,)),
            dma((2, 2, 7)),
            dma((2, 2, 7)),
            dma((18,)),
            dma((18,)),
        ],
        compiler_params=pltpu.CompilerParams(
            collective_id=0, has_side_effects=True, vmem_limit_bytes=63 * 1024 * 1024
        ),
    )(hid, ids, aff, gain.reshape(2, 1, half), gate, up, down, sgate, sup, sdown)


def solution(mesh):
    in_specs = (
        P(("node", "local"), None),
        P(("node", "local"), None),
        P(("node", "local"), None),
        P(),
        P(("node", "local"), None, None),
        P(("node", "local"), None, None),
        P("node", None, "local"),
        P(None, "local"),
        P(None, "local"),
        P(None, "local"),
    )
    return jax.shard_map(
        body, mesh=mesh, in_specs=in_specs, out_specs=P("node", "local"), check_vma=False
    )
```
